256 devices in a mesh: gx: 32 (over x, y, core), gy: 8 (over z).
Axes of the slice: x: 4, y: 4, z: 8, core: 2. Of those that a mesh axis runs over, the one named last changes fastest.
Arguments:
- points_x: bfloat16 [32, 16, 512, 256], P('gx', 'gy'), may hold values from -6 to 6
- near_tiles: bfloat16 [32, 16, 5, 512, 512], P('gx', 'gy'), may hold values from -0.09375 to 0.09375
- scales: float32 [32, 16, 5, 512], P('gx', 'gy'), may hold values from 0.25 to 4
- slot_direction: int32 [32, 16, 5], P('gx', 'gy'), may hold values from 0 to 4, each once within a row
- basis: bfloat16 [32, 16, 512, 256], P('gx', 'gy'), may hold values from -6 to 6
- leaf_transfer: float32 [32, 16, 256, 256], P('gx', 'gy'), may hold values from -1 to 2
- node_transfer: float32 [32, 8, 128, 256], P('gx', 'gy'), may hold values from -1 to 2
Outputs:
- near_field: bfloat16 [32, 16, 512, 256], P('gx', 'gy')
- leaf_q: bfloat16 [32, 16, 512, 256], P('gx', 'gy')
- top_factor: float32 [32, 8, 256, 256], P('gx', 'gy')
The draws below stay inside these ranges and needn't reach their ends.
Inputs may be any that keep to these rules, and one draw needn't show every extreme that they name: `slot_direction`: each leaf's row names each of the five directions once.
All inputs are finite; a program needn't handle non-finite values.
Results may differ from the reference program's by a relative error of at most 0.0065.
Values may be sent and summed in bfloat16 or wider, within the bound.
No kernel may reach another device: no remote copies, remote signals or barrier semaphores. Data moves between devices by JAX's collectives and lax.ppermute only.
A program may use at most 128 MiB of HBM per device.

```python
import math
import jax
import jax.numpy as jnp
from jax import lax

LEAF_PTS = 512
VECS = 256
RANK = 256
DEV_X = 32
DEV_Y = 8
LEAVES_X = 32
LEAVES_Y = 16
HALF_RANK = 128


def noise_part(key, shape):
    values = jnp.clip(jax.random.normal(key, shape, jnp.float32), -4.0, 4.0)
    return values * (0.25 / math.sqrt(RANK))


def draw_leaf_transfer(key, part):
    shape = (LEAVES_X, LEAVES_Y, RANK, RANK)
    identity = jnp.eye(RANK, dtype=jnp.float32)
    return identity[None, None] + noise_part(key, shape)


def draw_node_transfer(key, part):
    shape = (DEV_X, DEV_Y, HALF_RANK, RANK)
    parity = jnp.arange(DEV_X, dtype=jnp.int32) % 2
    row_index = parity[:, None] * HALF_RANK + jnp.arange(HALF_RANK, dtype=jnp.int32)[None, :]
    identity = (row_index[:, :, None] == jnp.arange(RANK, dtype=jnp.int32)[None, None, :]).astype(jnp.float32)
    return identity[:, None] + noise_part(key, shape)


def level_of(rng, extent, shards, smallest, largest):
    level = 1.0
    for position, shards_of in shards:
        steps = jax.random.uniform(jax.random.fold_in(jax.random.fold_in(rng, 6), position), (shards_of,), jnp.float32, smallest / len(shards), largest / len(shards))
        level = level * jnp.repeat(jnp.exp(steps), extent[position] // shards_of).reshape((-1,) + (1,) * (len(extent) - 1 - position))
    return level


def centred(stream_key, shape, spread, reach, split=(), kind=jnp.bfloat16):
    factor_of = level_of(stream_key, shape, split, -0.22, 0.18) if split else 1.0
    array = jax.random.normal(stream_key, shape, jnp.float32) * spread * factor_of
    return jnp.minimum(jnp.maximum(array, -reach), reach).astype(kind)


def setup_inputs(seed: int = 0) -> dict:
    key_list = jax.random.split(jax.random.key(seed), 8)
    return {
        "points_x": centred(key_list[0], (LEAVES_X, LEAVES_Y, LEAF_PTS, VECS), 1.0, 6.0, ((0, 32), (1, 8))),
        "near_tiles": centred(key_list[1], (LEAVES_X, LEAVES_Y, 5, LEAF_PTS, LEAF_PTS), (9 * LEAF_PTS) ** -0.5, 0.09375, ((0, 32), (1, 8))),
        "scales": jnp.clip(jnp.exp(math.log(4.0) - 2.7725887 * jax.random.uniform(key_list[2], (LEAVES_X, LEAVES_Y, 5, LEAF_PTS), jnp.float32) ** level_of(key_list[2], (LEAVES_X, LEAVES_Y, 5, LEAF_PTS), ((0, 32), (1, 8)), -0.2, 0.2)), 0.25, 4.0),
        "slot_direction": jax.vmap(lambda own: jax.random.permutation(own, 5))(jax.random.split(key_list[3], LEAVES_X * LEAVES_Y)).reshape((LEAVES_X, LEAVES_Y, 5)).astype(jnp.int32),
        "basis": centred(key_list[4], (LEAVES_X, LEAVES_Y, LEAF_PTS, RANK), 1.0, 6.0, ((0, 32), (1, 8))),
        "leaf_transfer": draw_leaf_transfer(jax.random.fold_in(key_list[7], 71), 0),
        "node_transfer": draw_node_transfer(jax.random.fold_in(key_list[7], 71), 0),
    }


def pick_directions(tiles_col, slots_col, scales_col):
    order_idx = jnp.argsort(slots_col, axis=-1).astype(jnp.int32)
    dir_tiles = jnp.take_along_axis(tiles_col, order_idx[:, :, None, None], axis=1)
    dir_scales = jnp.take_along_axis(scales_col, order_idx[:, :, None], axis=1)
    return (dir_tiles, dir_scales)

def shift_down(values):
    return jnp.concatenate([jnp.zeros_like(values[:1]), values[:-1]], axis=0)

def upper_cholesky(matrix):
    return jnp.swapaxes(jnp.linalg.cholesky(matrix), -1, -2)

def reference(points_x, near_tiles, scales, slot_direction, basis, leaf_transfer, node_transfer):
    highest = lax.Precision.HIGHEST
    leaves_x = points_x.shape[0]
    leaves_y = points_x.shape[1]
    padded = jnp.pad(points_x, ((1, 1), (1, 1), (0, 0), (0, 0)))

    def column_data(index):
        safe_index = jnp.clip(index, 0, leaves_x - 1).astype(jnp.int32)
        tiles_col = lax.dynamic_index_in_dim(near_tiles, safe_index, 0, keepdims=False)
        slots_col = lax.dynamic_index_in_dim(slot_direction, safe_index, 0, keepdims=False)
        scales_col = lax.dynamic_index_in_dim(scales, safe_index, 0, keepdims=False)
        return pick_directions(tiles_col, slots_col, scales_col)

    def incoming(tiles_col, scales_col, points_col, direction):
        scaled_x = (scales_col[:, direction, :, None] * points_col.astype(jnp.float32)).astype(jnp.bfloat16)
        scaled_x = lax.optimization_barrier(scaled_x).astype(jnp.float32)
        return jnp.einsum('lqp,lqv->lpv', tiles_col[:, direction].astype(jnp.float32), scaled_x, precision=highest)

    def column_terms(column):
        window = lax.dynamic_slice_in_dim(padded, column, 3, 0)
        west_col, own_col, east_col = (window[0], window[1], window[2])
        tiles_own, scales_own = column_data(column)
        tiles_west, scales_west = column_data(column - 1)
        tiles_east, scales_east = column_data(column + 1)
        operands = jnp.stack([own_col[1:-1], east_col[1:-1], own_col[2:], east_col[2:], west_col[2:]], axis=1)
        direct = jnp.einsum('ldpq,ldqv->ldpv', tiles_own.astype(jnp.float32), operands.astype(jnp.float32), precision=highest)
        direct = jnp.sum(direct * scales_own[..., None], axis=1)
        from_west = incoming(tiles_west, scales_west, west_col[1:-1], 1)
        from_west = from_west + shift_down(incoming(tiles_west, scales_west, west_col[1:-1], 3))
        from_own = shift_down(incoming(tiles_own, scales_own, own_col[1:-1], 2))
        from_east = shift_down(incoming(tiles_east, scales_east, east_col[1:-1], 4))
        return (direct + from_west + from_own + from_east).astype(jnp.bfloat16)
    near_field = lax.map(column_terms, jnp.arange(leaves_x, dtype=jnp.int32))
    basis_f = basis.astype(jnp.float32)
    points_count = basis.shape[2]
    rank = basis.shape[3]
    gram_leaf = jnp.einsum('abpi,abpj->abij', basis_f, basis_f, precision=highest) / points_count
    lower_leaf = jnp.linalg.cholesky(gram_leaf)
    factor_leaf = jnp.swapaxes(lower_leaf, -1, -2)
    leaf_q = lax.linalg.triangular_solve(lower_leaf, basis_f, left_side=False, lower=True, transpose_a=True)
    leaf_q = leaf_q.astype(jnp.bfloat16)
    moved_leaf = jnp.einsum('abij,abjk->abik', factor_leaf, leaf_transfer, precision=highest)
    grouped = moved_leaf.reshape(leaves_x // 2, 2, leaves_y // 2, 2, rank, rank)
    gram_one = 0.25 * jnp.einsum('aubvki,aubvkj->abij', grouped, grouped, precision=highest)
    factor_one = upper_cholesky(gram_one)
    half_rank = node_transfer.shape[2]
    dev_y = node_transfer.shape[1]
    transfer_one = node_transfer.reshape(leaves_x // 2, 2, dev_y, half_rank, rank)
    transfer_one = jnp.transpose(transfer_one, (0, 2, 1, 3, 4)).reshape(leaves_x // 2, dev_y, rank, rank)
    moved_one = jnp.einsum('abij,abjk->abik', factor_one, transfer_one, precision=highest)
    grouped_one = moved_one.reshape(leaves_x // 4, 2, dev_y // 2, 2, rank, rank)
    gram_two = 0.25 * jnp.einsum('aubvki,aubvkj->abij', grouped_one, grouped_one, precision=highest)
    factor_two = upper_cholesky(gram_two)
    top_factor = jnp.repeat(jnp.repeat(factor_two, 4, axis=0), 2, axis=1)
    return (near_field, leaf_q, top_factor)
```

```python
import jax
import jax.numpy as jnp
from jax import lax
from jax.experimental import pallas as pl
from jax.experimental.pallas import tpu as pltpu
from jax.sharding import PartitionSpec as P

F32 = jnp.float32
BF16 = jnp.bfloat16
ANY = pl.BlockSpec(memory_space=pl.ANY)
VMEM = pl.BlockSpec(memory_space=pltpu.VMEM)
SMEM = pl.BlockSpec(memory_space=pltpu.SMEM)
PANEL = 32
PIECE = 16


def dot(a, b, dims, precision=lax.Precision.HIGHEST):
    return lax.dot_general(a, b, (dims, ((), ())), precision=precision, preferred_element_type=F32)


def nn(a, b):
    return dot(a, b, ((1,), (0,)))


def tn(a, b):
    return dot(a, b, ((0,), (0,)))


def bf_nn(a, b):
    return dot(a, b, ((1,), (0,)), lax.Precision.DEFAULT)


def bf_nt(a, b):
    return dot(a, b, ((1,), (1,)), lax.Precision.DEFAULT)


def swap(block, axes, sizes, partner):
    count_x, count_y = sizes
    route = []
    for i in range(count_x):
        for j in range(count_y):
            x, y = partner(i, j)
            if 0 <= x < count_x and 0 <= y < count_y:
                route.append((i * count_y + j, x * count_y + y))
    return lax.ppermute(block, axes, route)


def panel_step(k, tiles, nb, sb):
    iota = lax.broadcasted_iota(jnp.int32, (8, 128), 0)
    groups = nb // 8
    scale = [jnp.ones((8, 128), F32) for _ in range(groups)]
    for s in range(0, nb, sb):
        base = (k + s) % 128
        g0 = s // 8
        cols = []
        for j in range(sb):
            cols.append(
                {
                    g: jnp.broadcast_to(tiles[g][0][:, base + j : base + j + 1], (8, 128))
                    for g in range(g0 + j // 8, groups)
                }
            )
        for p in range(sb):
            gp = g0 + p // 8
            r = p % 8
            pivot = jnp.broadcast_to(cols[p][gp][r : r + 1, :], (8, 128))
            inv = 1.0 / pivot
            scale[gp] = jnp.where(iota == r, lax.rsqrt(pivot), scale[gp])
            for j in range(p + 1, sb):
                gj = g0 + j // 8
                t = jnp.broadcast_to(cols[p][gj][j % 8 : j % 8 + 1, :], (8, 128)) * inv
                for g in range(gj, groups):
                    cols[j][g] = cols[j][g] - cols[p][g] * t
            rows = [jnp.broadcast_to(t[r : r + 1, :], (8, 128)) * inv for t in tiles[gp]]
            for g in range(gp, groups):
                c = cols[p][g]
                if g == gp:
                    if r == 7:
                        continue
                    c = jnp.where(iota > r, c, 0.0)
                tiles[g] = [t - c * w for t, w in zip(tiles[g], rows)]
    return [[t * scale[g] for t in tiles[g]] for g in range(groups)]


def factorize(reads, u_refs, w_refs, n):
    lanes = lax.broadcasted_iota(jnp.int32, (8, 128), 1)
    sub = lax.broadcasted_iota(jnp.int32, (8, 128), 0)
    nb = PANEL
    for k in range(0, n, nb):
        lo = k // 128 * 128
        hi = (k + nb - 1) // 128 * 128 + 128
        for read, u, w in zip(reads, u_refs, w_refs):
            main = read(slice(k, k + nb), slice(lo, n))
            side = jnp.zeros((nb, hi), F32)
            if k:
                col = u[0:k, k : k + nb]
                main = main - tn(col, u[0:k, lo:n])
                if w is not None:
                    side = -tn(col, w[0:k, 0:hi])
            tiles = []
            for g in range(nb // 8):
                row = [main[8 * g : 8 * g + 8, c : c + 128] for c in range(0, n - lo, 128)]
                if w is not None:
                    more = [side[8 * g : 8 * g + 8, c : c + 128] for c in range(0, hi, 128)]
                    more[-1] = more[-1] + jnp.where(lanes == sub + (k + 8 * g - (hi - 128)), 1.0, 0.0)
                    row += more
                tiles.append(row)
            tiles = panel_step(k, tiles, nb, PIECE)
            na = (n - lo) // 128
            for g in range(nb // 8):
                first = k + 8 * g
                r = slice(first, first + 8)
                for i in range(na):
                    c = lo + 128 * i
                    t = tiles[g][i]
                    if c == lo:
                        t = jnp.where(lanes + c >= sub + first, t, 0.0)
                    u[r, c : c + 128] = t
                for c in range(0, lo, 128):
                    u[r, c : c + 128] = jnp.zeros((8, 128), F32)
                if w is not None:
                    for i, c in enumerate(range(0, hi, 128)):
                        w[r, c : c + 128] = tiles[g][na + i]
                    for c in range(hi, n, 128):
                        w[r, c : c + 128] = jnp.zeros((8, 128), F32)


def gram_kernel(basis, transfer, node, gram, sent):
    points = basis.shape[2]
    total = None
    for leaf in range(2):
        b = basis[0, leaf]
        g = dot(b, b, ((0,), (0,)), lax.Precision.DEFAULT) / points
        gram[leaf] = g
        t = transfer[0, leaf]
        part = tn(t, nn(g, t))
        total = part if total is None else total + part
    rank = total.shape[0]
    sent[0:rank, :] = total
    sent[rank : rank + node.shape[2], :] = node[0, 0]


def node_kernel(own, other, out, stacked):
    rank = own.shape[1]
    half = rank // 2
    parity = lax.axis_index("gx") % 2
    gram = 0.25 * (own[0:rank, :] + other[0:rank, :])
    mine = pl.multiple_of(parity * half, half)
    theirs = pl.multiple_of((1 - parity) * half, half)
    stacked[pl.ds(mine, half), :] = own[rank : rank + half, :]
    stacked[pl.ds(theirs, half), :] = other[rank : rank + half, :]
    t = stacked[...]
    out[...] = 0.25 * tn(t, nn(gram, t))


def leaf_kernel(gram, basis, q, u, w):
    n = gram.shape[1]
    reads = [lambda r, c, m=m: gram[m, r, c] for m in range(2)]
    factorize(reads, [u.at[m] for m in range(2)], [w.at[m] for m in range(2)], n)
    for leaf in range(2):
        rest = w[leaf]
        total = None
        for _ in range(3):
            part = rest.astype(BF16)
            rest = rest - part.astype(F32)
            term = bf_nt(basis[0, leaf], part)
            total = term if total is None else total + term
        q[0, leaf] = total.astype(BF16)


def top_kernel(own, other, out):
    n = own.shape[0]
    factorize([lambda r, c: own[r, c] + other[r, c]], [out.at[0, 0]], [None], n)


def slot_of(slots, leaf, direction):
    found = 0
    for s in range(5):
        found = found + jnp.where(slots[0, leaf, s] == direction, s, 0)
    return found


def scale_row(scales, slots, leaf, direction):
    return scales[0, leaf, pl.ds(slot_of(slots, leaf, direction), 1), :]


def mirror_kernel(slots, points, scales, tiles, acc, gx_a, gx_b, ns_a, ns_b, ne_a, ne_b, nw_a, nw_b,
                  held, xt, east, west, up, tile_sems, out_sems):
    order = [(0, 2), (0, 1), (0, 3), (0, 4), (1, 1), (1, 2), (1, 3), (1, 4), (0, 0), (1, 0)]
    copies = {}
    for leaf, d in order:
        place = leaf * 5 + d
        copies[leaf, d] = pltpu.make_async_copy(
            tiles.at[0, leaf, slot_of(slots, leaf, d)], held.at[place], tile_sems.at[place]
        )
        copies[leaf, d].start()
    for leaf in range(2):
        xt[leaf] = points[0, leaf].T
    even_x = lax.axis_index("gx") % 2 == 0
    even_y = lax.axis_index("gy") % 2 == 0
    waits = []

    def out_pair(first, second, a, b, even):
        one, two = out_sems.at[len(waits)], out_sems.at[len(waits) + 1]

        @pl.when(even)
        def _():
            pltpu.make_async_copy(first, a, one).start()
            pltpu.make_async_copy(second, b, two).start()

        @pl.when(jnp.logical_not(even))
        def _():
            pltpu.make_async_copy(second, a, one).start()
            pltpu.make_async_copy(first, b, two).start()

        waits.append(pltpu.make_async_copy(first, a, one))
        waits.append(pltpu.make_async_copy(second, b, two))

    def mirrored(leaf, d):
        copies[leaf, d].wait()
        scaled = (xt[leaf].astype(F32) * scale_row(scales, slots, leaf, d)).astype(BF16)
        return bf_nn(scaled, held[leaf * 5 + d])

    def direct(leaf, d, x):
        return bf_nt(x, held[leaf * 5 + d]) * scale_row(scales, slots, leaf, d)

    acc[1] = mirrored(0, 2)
    acc[0] = direct(0, 2, xt[1])
    east[0] = mirrored(0, 1).astype(BF16)
    east_one = mirrored(0, 3)
    west[0] = mirrored(0, 4).astype(BF16)
    east[1] = (east_one + mirrored(1, 1)).astype(BF16)
    east[2] = xt[1]
    west[1] = xt[0]
    west[2] = xt[1]
    out_pair(east, west, gx_a, gx_b, even_x)
    for i, (a, b) in enumerate(((ns_a, ns_b), (ne_a, ne_b), (nw_a, nw_b))):
        up[i] = mirrored(1, 2 + i).astype(BF16)
        out_pair(up.at[i], xt.at[0], a, b, even_y)
    for leaf in range(2):
        copies[leaf, 0].wait()
        acc[leaf] += direct(leaf, 0, xt[leaf])
    for w in waits:
        w.wait()


def near_kernel(slots, scales, tiles, acc, gx_a, gx_b, ns_a, ns_b, ne_a, ne_b, nw_a, nw_b, out,
                held, east, west, north, south, tile_sems, in_sems):
    order = [(0, 1), (0, 3), (0, 4), (1, 1), (1, 2), (1, 3), (1, 4)]
    even_x = lax.axis_index("gx") % 2 == 0
    even_y = lax.axis_index("gy") % 2 == 0
    waits = []

    def in_pair(first, second, a, b, even):
        one, two = in_sems.at[len(waits)], in_sems.at[len(waits) + 1]

        @pl.when(even)
        def _():
            pltpu.make_async_copy(a, first, one).start()
            pltpu.make_async_copy(b, second, two).start()

        @pl.when(jnp.logical_not(even))
        def _():
            pltpu.make_async_copy(b, first, one).start()
            pltpu.make_async_copy(a, second, two).start()

        waits.append(pltpu.make_async_copy(a, first, one))
        waits.append(pltpu.make_async_copy(b, second, two))

    in_pair(east, west, gx_a, gx_b, even_x)
    copies = {}
    for leaf, d in order:
        place = leaf * 5 + d
        copies[leaf, d] = pltpu.make_async_copy(
            tiles.at[0, leaf, slot_of(slots, leaf, d)], held.at[place], tile_sems.at[place]
        )
        copies[leaf, d].start()
    for i, (a, b) in enumerate(((ns_a, ns_b), (ne_a, ne_b), (nw_a, nw_b))):
        in_pair(north.at[i], south.at[i], a, b, even_y)
    for w in waits:
        w.wait()

    def direct(leaf, d, x):
        copies[leaf, d].wait()
        return bf_nt(x, held[leaf * 5 + d]) * scale_row(scales, slots, leaf, d)

    low = acc[0] + west[0].astype(F32)
    for i in range(3):
        low = low + south[i].astype(F32)
    low = low + direct(0, 1, east[1])
    low = low + direct(0, 3, east[2])
    low = low + direct(0, 4, west[2])
    out[0, 0] = low.T.astype(BF16)
    high = acc[1] + west[1].astype(F32) + east[0].astype(F32)
    high = high + direct(1, 1, east[2])
    for i in range(3):
        high = high + direct(1, 2 + i, north[i])
    out[0, 1] = high.T.astype(BF16)


def shape(*dims, dtype=BF16):
    return jax.ShapeDtypeStruct(dims, dtype)


def call(kernel, outs, in_specs, out_specs, scratch=(), flops=0, moved=0):
    return pl.pallas_call(
        kernel,
        out_shape=outs,
        in_specs=in_specs,
        out_specs=out_specs,
        scratch_shapes=list(scratch),
        compiler_params=pltpu.CompilerParams(vmem_limit_bytes=48 << 20),
        cost_estimate=pl.CostEstimate(flops=flops, bytes_accessed=moved, transcendentals=0),
    )


def make_shards(sizes):
    axes = ("gx", "gy")

    def shards(points_x, near_tiles, scales, slot_direction, basis, leaf_transfer, node_transfer):
        pts, vecs = points_x.shape[2:]
        rank = basis.shape[3]
        half = node_transfer.shape[2]
        dma = pltpu.SemaphoreType.DMA

        gram, sent = call(
            gram_kernel,
            (shape(2, rank, rank, dtype=F32), shape(rank + half, rank, dtype=F32)),
            [VMEM] * 3,
            (VMEM, VMEM),
            flops=10**9,
            moved=4 << 20,
        )(basis, leaf_transfer, node_transfer)
        got = swap(sent, axes, sizes, lambda i, j: (i ^ 1, j))

        block = shape(vecs, pts)
        trio = shape(3, vecs, pts)
        acc, *outgoing = call(
            mirror_kernel,
            (shape(2, vecs, pts, dtype=F32), trio, trio, *[block] * 6),
            [SMEM, VMEM, VMEM, ANY],
            (VMEM, *[ANY] * 8),
            [
                pltpu.VMEM((10, pts, pts), BF16),
                pltpu.VMEM((2, vecs, pts), BF16),
                pltpu.VMEM((3, vecs, pts), BF16),
                pltpu.VMEM((3, vecs, pts), BF16),
                pltpu.VMEM((3, vecs, pts), BF16),
                dma((10,)),
                dma((8,)),
            ],
            flops=3 * 10**9,
            moved=10 << 20,
        )(slot_direction, points_x, scales, near_tiles)

        node = call(node_kernel, shape(rank, rank, dtype=F32), [VMEM] * 2, VMEM,
                    [pltpu.VMEM((rank, rank), F32)], flops=10**9, moved=2 << 20)(sent, got)
        pair = node + swap(node, axes, sizes, lambda i, j: (i ^ 2, j))
        other = swap(pair, axes, sizes, lambda i, j: (i, j ^ 1))

        def across(parity, first):
            return lambda i, j: first(i, j, 1 if (j % 2 == 0) == (parity == 0) else -1)

        incoming = []
        for parity in range(2):
            incoming.append(
                swap(outgoing[parity], axes, sizes,
                     lambda i, j, q=parity: (i + (1 if (i % 2 == 0) == (q == 0) else -1), j))
            )
        for turn, side in enumerate((0, 1, -1)):
            for parity in range(2):
                incoming.append(
                    swap(outgoing[2 + 2 * turn + parity], axes, sizes,
                         across(parity, lambda i, j, step, side=side: (i + side * step, j + step)))
                )

        leaf_q = call(
            leaf_kernel,
            shape(*basis.shape),
            [VMEM] * 2,
            VMEM,
            [pltpu.VMEM((2, rank, rank), F32), pltpu.VMEM((2, rank, rank), F32)],
            flops=12 * 10**9,
            moved=4 << 20,
        )(gram, basis)

        top = call(top_kernel, shape(1, 1, rank, rank, dtype=F32), [VMEM] * 2, VMEM, flops=8 * 10**9,
                   moved=1 << 20)(pair, other)

        near = call(
            near_kernel,
            shape(*points_x.shape),
            [SMEM, VMEM, ANY, VMEM, *[ANY] * 8],
            VMEM,
            [
                pltpu.VMEM((10, pts, pts), BF16),
                *[pltpu.VMEM((3, vecs, pts), BF16)] * 4,
                dma((10,)),
                dma((8,)),
            ],
            flops=3 * 10**9,
            moved=10 << 20,
        )(slot_direction, scales, near_tiles, acc, *incoming)
        return near, leaf_q, top

    return shards


def solution(mesh):
    leaf = P("gx", "gy", None, None)
    placed = (leaf, P("gx", "gy", None, None, None), leaf, P("gx", "gy", None), leaf, leaf, leaf)
    return jax.shard_map(
        make_shards((mesh.shape["gx"], mesh.shape["gy"])),
        mesh=mesh,
        in_specs=placed,
        out_specs=(leaf, leaf, leaf),
        check_vma=False,
    )
```

```python
import jax
import jax.numpy as jnp
from jax import lax
from jax.experimental import pallas as pl
from jax.experimental.pallas import tpu as pltpu
from jax.sharding import PartitionSpec as P

F32 = jnp.float32
BF16 = jnp.bfloat16
ANY = pl.BlockSpec(memory_space=pl.ANY)
VMEM = pl.BlockSpec(memory_space=pltpu.VMEM)
SMEM = pl.BlockSpec(memory_space=pltpu.SMEM)
PANEL = 32
PIECE = 16


def dot(a, b, dims, precision=lax.Precision.HIGHEST):
    return lax.dot_general(a, b, (dims, ((), ())), precision=precision, preferred_element_type=F32)


def nn(a, b):
    return dot(a, b, ((1,), (0,)))


def tn(a, b):
    return dot(a, b, ((0,), (0,)))


def bf_nn(a, b):
    return dot(a, b, ((1,), (0,)), lax.Precision.DEFAULT)


def bf_nt(a, b):
    return dot(a, b, ((1,), (1,)), lax.Precision.DEFAULT)


def send(block, axes, sizes, partner):
    count_x, count_y = sizes
    route = []
    for i in range(count_x):
        for j in range(count_y):
            x, y = partner(i, j)
            route.append((i * count_y + j, x % count_x * count_y + y % count_y))
    return lax.ppermute(block, axes, route)


def panel_step(k, tiles, nb, sb):
    iota = lax.broadcasted_iota(jnp.int32, (8, 128), 0)
    groups = nb // 8
    scale = [jnp.ones((8, 128), F32) for _ in range(groups)]
    for s in range(0, nb, sb):
        base = (k + s) % 128
        g0 = s // 8
        cols = []
        for j in range(sb):
            cols.append(
                {
                    g: jnp.broadcast_to(tiles[g][0][:, base + j : base + j + 1], (8, 128))
                    for g in range(g0 + j // 8, groups)
                }
            )
        for p in range(sb):
            gp = g0 + p // 8
            r = p % 8
            pivot = jnp.broadcast_to(cols[p][gp][r : r + 1, :], (8, 128))
            inv = 1.0 / pivot
            scale[gp] = jnp.where(iota == r, lax.rsqrt(pivot), scale[gp])
            for j in range(p + 1, sb):
                gj = g0 + j // 8
                t = jnp.broadcast_to(cols[p][gj][j % 8 : j % 8 + 1, :], (8, 128)) * inv
                for g in range(gj, groups):
                    cols[j][g] = cols[j][g] - cols[p][g] * t
            rows = [jnp.broadcast_to(t[r : r + 1, :], (8, 128)) * inv for t in tiles[gp]]
            for g in range(gp, groups):
                c = cols[p][g]
                if g == gp:
                    if r == 7:
                        continue
                    c = jnp.where(iota > r, c, 0.0)
                tiles[g] = [t - c * w for t, w in zip(tiles[g], rows)]
    return [[t * scale[g] for t in tiles[g]] for g in range(groups)]


def factorize(reads, u_refs, w_refs, n):
    lanes = lax.broadcasted_iota(jnp.int32, (8, 128), 1)
    sub = lax.broadcasted_iota(jnp.int32, (8, 128), 0)
    nb = PANEL
    for k in range(0, n, nb):
        lo = k // 128 * 128
        hi = (k + nb - 1) // 128 * 128 + 128
        for read, u, w in zip(reads, u_refs, w_refs):
            main = read(slice(k, k + nb), slice(lo, n))
            side = jnp.zeros((nb, hi), F32)
            if k:
                col = u[0:k, k : k + nb]
                main = main - tn(col, u[0:k, lo:n])
                if w is not None:
                    side = -tn(col, w[0:k, 0:hi])
            tiles = []
            for g in range(nb // 8):
                row = [main[8 * g : 8 * g + 8, c : c + 128] for c in range(0, n - lo, 128)]
                if w is not None:
                    more = [side[8 * g : 8 * g + 8, c : c + 128] for c in range(0, hi, 128)]
                    more[-1] = more[-1] + jnp.where(lanes == sub + (k + 8 * g - (hi - 128)), 1.0, 0.0)
                    row += more
                tiles.append(row)
            tiles = panel_step(k, tiles, nb, PIECE)
            na = (n - lo) // 128
            for g in range(nb // 8):
                first = k + 8 * g
                r = slice(first, first + 8)
                for i in range(na):
                    c = lo + 128 * i
                    t = tiles[g][i]
                    if c == lo:
                        t = jnp.where(lanes + c >= sub + first, t, 0.0)
                    u[r, c : c + 128] = t
                for c in range(0, lo, 128):
                    u[r, c : c + 128] = jnp.zeros((8, 128), F32)
                if w is not None:
                    for i, c in enumerate(range(0, hi, 128)):
                        w[r, c : c + 128] = tiles[g][na + i]
                    for c in range(hi, n, 128):
                        w[r, c : c + 128] = jnp.zeros((8, 128), F32)


def node_kernel(own, other, out, stacked):
    rank = own.shape[1]
    half = rank // 2
    parity = lax.axis_index("gx") % 2
    gram = 0.25 * (own[0:rank, :] + other[0:rank, :])
    mine = pl.multiple_of(parity * half, half)
    theirs = pl.multiple_of((1 - parity) * half, half)
    stacked[pl.ds(mine, half), :] = own[rank : rank + half, :]
    stacked[pl.ds(theirs, half), :] = other[rank : rank + half, :]
    t = stacked[...]
    out[...] = 0.25 * tn(t, nn(gram, t))


def leaf_kernel(gram, basis, q, u, w):
    n = gram.shape[1]
    reads = [lambda r, c, m=m: gram[m, r, c] for m in range(2)]
    factorize(reads, [u.at[m] for m in range(2)], [w.at[m] for m in range(2)], n)
    for leaf in range(2):
        rest = w[leaf]
        total = None
        for _ in range(3):
            part = rest.astype(BF16)
            rest = rest - part.astype(F32)
            term = bf_nt(basis[0, leaf], part)
            total = term if total is None else total + term
        q[0, leaf] = total.astype(BF16)


def top_kernel(own, other, out):
    n = own.shape[0]
    factorize([lambda r, c: own[r, c] + other[r, c]], [out.at[0, 0]], [None], n)


def slot_of(slots, leaf, direction):
    found = 0
    for s in range(5):
        found = found + jnp.where(slots[0, leaf, s] == direction, s, 0)
    return found


def first_kernel(basis_h, transfer_h, node_h, slots_h, points_h, scales_h, tiles_h,
                 gram_h, sent_h, low_h, high_h, up_h, x_h, gx_a, gx_b,
                 gram, sent, acc, basis, transfer, slots, points, scales, tiles, east, west, in_sems, tile_sems, out_sems):
    rank = gram.shape[1]
    half = node_h.shape[2]
    sources = (
        (basis_h, basis), (transfer_h, transfer), (slots_h, slots), (points_h, points), (scales_h, scales),
        (node_h.at[0, 0], sent.at[pl.ds(rank, half)]),
    )
    loads = [pltpu.make_async_copy(a, b, in_sems.at[i]) for i, (a, b) in enumerate(sources)]
    for load in loads:
        load.start()

    def tile_copy(leaf, slot):
        return pltpu.make_async_copy(tiles_h.at[0, leaf, slot], tiles.at[leaf, slot], tile_sems.at[leaf, slot])

    for leaf in range(2):
        for slot in range(5):
            tile_copy(leaf, slot).start()

    loads[0].wait()
    loads[1].wait()
    total = None
    for leaf in range(2):
        b = basis[0, leaf]
        g = dot(b, b, ((0,), (0,)), lax.Precision.DEFAULT) / basis.shape[2]
        gram[leaf] = g
        t = transfer[0, leaf]
        part = tn(t, nn(g, t))
        total = part if total is None else total + part
    sent[0:rank, :] = total
    for load in loads[2:]:
        load.wait()
    waits = []

    def store(scratch, target):
        waits.append(pltpu.make_async_copy(scratch, target, out_sems.at[len(waits)]))
        waits[-1].start()

    store(gram, gram_h)
    store(sent, sent_h)
    west[0] = points[0, 0].T
    west[3] = points[0, 1].T
    east[3] = west[3]
    xt = (west.at[0], west.at[3])
    store(west.at[0], x_h)
    for leaf in range(2):
        for slot in range(5):
            tile_copy(leaf, slot).wait()

    def mirrored(leaf, d):
        slot = slot_of(slots, leaf, d)
        scaled = (xt[leaf][...].astype(F32) * scales[0, slot, pl.ds(leaf, 1), :]).astype(BF16)
        return bf_nn(scaled, tiles[leaf, slot])

    def direct(leaf, d, x):
        slot = slot_of(slots, leaf, d)
        return bf_nt(x, tiles[leaf, slot]) * scales[0, slot, pl.ds(leaf, 1), :]

    east[0] = mirrored(0, 1).astype(BF16)
    west[1] = mirrored(0, 4).astype(BF16)
    east[1] = (mirrored(0, 3) + mirrored(1, 1)).astype(BF16)
    east[2] = mirrored(1, 3).astype(BF16)
    west[2] = mirrored(1, 4).astype(BF16)
    even = lax.axis_index("gx") % 2 == 0

    @pl.when(even)
    def _():
        pltpu.make_async_copy(east, gx_a, out_sems.at[3]).start()
        pltpu.make_async_copy(west, gx_b, out_sems.at[4]).start()

    @pl.when(jnp.logical_not(even))
    def _():
        pltpu.make_async_copy(west, gx_a, out_sems.at[3]).start()
        pltpu.make_async_copy(east, gx_b, out_sems.at[4]).start()

    waits.append(pltpu.make_async_copy(east, gx_a, out_sems.at[3]))
    waits.append(pltpu.make_async_copy(west, gx_b, out_sems.at[4]))
    acc[0] = mirrored(1, 2)
    store(acc.at[0], up_h)
    acc[1] = direct(0, 0, xt[0][...]) + direct(0, 2, xt[1][...])
    store(acc.at[1], low_h)
    acc[2] = direct(1, 0, xt[1][...]) + mirrored(0, 2)
    store(acc.at[2], high_h)
    for w in waits:
        w.wait()


def sides():
    gx, gy = lax.axis_index("gx"), lax.axis_index("gy")
    last_x, last_y = lax.axis_size("gx") - 1, lax.axis_size("gy") - 1
    return gx < last_x, gx > 0, gy < last_y, gy > 0, gx % 2 == 0


def kept(inside, product):
    return jnp.where(inside, product.astype(F32), 0.0)


def up_kernel(own, a, b, out):
    east, west, _, _, even = sides()
    out[...] = (own[...] + a[2].astype(F32) + kept(jnp.where(even, west, east), b[2])).astype(BF16)


def near_kernel(slots, scales, tiles_h, low_in, high_in, gx_a, gx_b, n, ne, nw, out, low_out, tiles, done, sems, done_sem):
    order = ((0, 1), (0, 3), (0, 4), (1, 1), (1, 2), (1, 3), (1, 4))

    def tile_copy(leaf, d):
        place = order.index((leaf, d))
        return pltpu.make_async_copy(tiles_h.at[0, leaf, slot_of(slots, leaf, d)], tiles.at[place], sems.at[place])

    for leaf, d in order:
        tile_copy(leaf, d).start()
    east, west, north, _, even = sides()
    beside = jnp.where(even, west, east)

    def from_east(i):
        return jnp.where(even, gx_a[i], gx_b[i])

    def from_west(i):
        return jnp.where(even, gx_b[i], gx_a[i])

    def direct(leaf, d, x, inside):
        tile_copy(leaf, d).wait()
        scale = jnp.where(inside, scales[0, slot_of(slots, leaf, d), pl.ds(leaf, 1), :], 0.0)
        return bf_nt(x, tiles[order.index((leaf, d))]) * scale

    x1_east = from_east(3)
    low = low_in[...] + kept(west, from_west(0)) + direct(0, 1, from_east(0), east)
    low = low + direct(0, 3, x1_east, east)
    low_out[...] = low + direct(0, 4, from_west(3), west)
    high = high_in[...] + gx_a[1].astype(F32) + kept(beside, gx_b[1]) + direct(1, 1, x1_east, east)
    high = high + direct(1, 2, n[...], north)
    high = high + direct(1, 3, ne[...], north & east)
    high = high + direct(1, 4, nw[...], north & west)
    done[...] = high.T.astype(BF16)
    copy = pltpu.make_async_copy(done, out.at[0, 1], done_sem)
    copy.start()
    copy.wait()


def last_kernel(near, low, south, out, done, sem):
    _, _, _, inside, _ = sides()
    done[...] = (low[...] + kept(inside, south[...])).T.astype(BF16)
    copy = pltpu.make_async_copy(done, out.at[0, 0], sem)
    copy.start()
    copy.wait()


def shape(*dims, dtype=BF16):
    return jax.ShapeDtypeStruct(dims, dtype)


def call(kernel, outs, in_specs, out_specs, scratch=(), flops=0, moved=0, vmem=48 << 20, aliases=None):
    return pl.pallas_call(
        kernel,
        out_shape=outs,
        in_specs=in_specs,
        out_specs=out_specs,
        scratch_shapes=list(scratch),
        input_output_aliases=aliases or {},
        compiler_params=pltpu.CompilerParams(vmem_limit_bytes=vmem),
        cost_estimate=pl.CostEstimate(flops=flops, bytes_accessed=moved, transcendentals=0),
    )


def make_shards(sizes):
    axes = ("gx", "gy")

    def shards(points_x, near_tiles, scales, slot_direction, basis, leaf_transfer, node_transfer):
        pts, vecs = points_x.shape[2:]
        rank = basis.shape[3]
        half = node_transfer.shape[2]
        dma = pltpu.SemaphoreType.DMA

        block = shape(vecs, pts)
        wide = shape(vecs, pts, dtype=F32)
        sides_sent = shape(4, vecs, pts)
        scales = jnp.transpose(scales, (0, 2, 1, 3))
        gram, sent, low, high, up, own_x, gx_a, gx_b = call(
            first_kernel,
            (
                shape(2, rank, rank, dtype=F32),
                shape(rank + half, rank, dtype=F32),
                wide, wide, wide, block, sides_sent, sides_sent,
            ),
            [ANY] * 7,
            (ANY,) * 8,
            [
                pltpu.VMEM((2, rank, rank), F32),
                pltpu.VMEM((rank + half, rank), F32),
                pltpu.VMEM((3, vecs, pts), F32),
                pltpu.VMEM(basis.shape, BF16),
                pltpu.VMEM(leaf_transfer.shape, F32),
                pltpu.SMEM(slot_direction.shape, jnp.int32),
                pltpu.VMEM(points_x.shape, BF16),
                pltpu.VMEM(scales.shape, F32),
                pltpu.VMEM(near_tiles.shape[1:], BF16),
                *[pltpu.VMEM((4, vecs, pts), BF16)] * 2,
                dma((6,)),
                dma((2, 5)),
                dma((8,)),
            ],
            flops=10**6,
            moved=1 << 10,
            vmem=32 << 20,
        )(*(pltpu.with_memory_space_constraint(a, pltpu.HBM) for a in (
            basis, leaf_transfer, node_transfer, slot_direction, points_x, scales, near_tiles)))
        got = send(sent, axes, sizes, lambda i, j: (i ^ 1, j))

        got_a = send(gx_a, axes, sizes, lambda i, j: (i ^ 1, j))
        got, got_a = lax.optimization_barrier((got, got_a))
        node = call(node_kernel, shape(rank, rank, dtype=F32), [VMEM] * 2, VMEM,
                    [pltpu.VMEM((rank, rank), F32)], flops=10**6, moved=1 << 10)(sent, got)
        node_got = send(node, axes, sizes, lambda i, j: (i ^ 2, j))
        got_b = send(gx_b, axes, sizes, lambda i, j: (i - 1 if i % 2 == 0 else i + 1, j))
        n = send(own_x, axes, sizes, lambda i, j: (i, j - 1))
        ne = send(own_x, axes, sizes, lambda i, j: (i - 1, j - 1))
        nw = send(own_x, axes, sizes, lambda i, j: (i + 1, j - 1))
        leaf_q = call(
            leaf_kernel,
            shape(*basis.shape),
            [VMEM] * 2,
            VMEM,
            [pltpu.VMEM((2, rank, rank), F32), pltpu.VMEM((2, rank, rank), F32)],
            flops=10**6,
            moved=1 << 10,
        )(gram, basis)

        leaf_q, node_got, got_b = lax.optimization_barrier((leaf_q, node_got, got_b))
        pair = node + node_got
        other = send(pair, axes, sizes, lambda i, j: (i, j ^ 1))
        total_up = call(up_kernel, block, [VMEM] * 3, VMEM, moved=1 << 10)(up, got_a, got_b)
        south = send(total_up, axes, sizes, lambda i, j: (i, j + 1))

        near, low = call(
            near_kernel,
            (shape(*points_x.shape), wide),
            [SMEM, VMEM, ANY, *[VMEM] * 7],
            (ANY, VMEM),
            [pltpu.VMEM((7, pts, pts), BF16), pltpu.VMEM((pts, vecs), BF16), dma((7,)), dma],
            flops=10**6,
            moved=1 << 10,
        )(slot_direction, scales, near_tiles, low, high, got_a, got_b, n, ne, nw)
        low, other = lax.optimization_barrier((low, other))
        top = call(top_kernel, shape(1, 1, rank, rank, dtype=F32), [VMEM] * 2, VMEM, flops=10**6,
                   moved=1 << 10)(pair, other)

        near = call(
            last_kernel,
            shape(*points_x.shape),
            [ANY, VMEM, VMEM],
            ANY,
            [pltpu.VMEM((pts, vecs), BF16), dma],
            moved=1 << 10,
            aliases={0: 0},
        )(near, low, south)
        return near, leaf_q, top

    return shards


def solution(mesh):
    leaf = P("gx", "gy", None, None)
    placed = (leaf, P("gx", "gy", None, None, None), leaf, P("gx", "gy", None), leaf, leaf, leaf)
    return jax.shard_map(
        make_shards((mesh.shape["gx"], mesh.shape["gy"])),
        mesh=mesh,
        in_specs=placed,
        out_specs=(leaf, leaf, leaf),
        check_vma=False,
    )
```

```python
import jax
import jax.numpy as jnp
from jax import lax
from jax.experimental import pallas as pl
from jax.experimental.pallas import tpu as pltpu
from jax.sharding import PartitionSpec as P

F32 = jnp.float32
BF16 = jnp.bfloat16
ANY = pl.BlockSpec(memory_space=pl.ANY)
VMEM = pl.BlockSpec(memory_space=pltpu.VMEM)
SMEM = pl.BlockSpec(memory_space=pltpu.SMEM)
PANEL = 32
PIECE = 16


def dot(a, b, dims, precision=lax.Precision.HIGHEST):
    return lax.dot_general(a, b, (dims, ((), ())), precision=precision, preferred_element_type=F32)


def nn(a, b):
    return dot(a, b, ((1,), (0,)))


def tn(a, b):
    return dot(a, b, ((0,), (0,)))


def bf_nn(a, b):
    return dot(a, b, ((1,), (0,)), lax.Precision.DEFAULT)


def bf_nt(a, b):
    return dot(a, b, ((1,), (1,)), lax.Precision.DEFAULT)


def send(block, axes, sizes, partner):
    count_x, count_y = sizes
    route = []
    for i in range(count_x):
        for j in range(count_y):
            x, y = partner(i, j)
            route.append((i * count_y + j, x % count_x * count_y + y % count_y))
    return lax.ppermute(block, axes, route)


def eliminate(jobs, nb, sb):
    iota = lax.broadcasted_iota(jnp.int32, (8, 128), 0)
    groups = nb // 8
    scales = [[jnp.ones((8, 128), F32) for _ in range(groups)] for _ in jobs]
    for s in range(0, nb, sb):
        g0 = s // 8
        columns = []
        for k, tiles in jobs:
            base = (k + s) % 128
            columns.append(
                [
                    {
                        g: jnp.broadcast_to(tiles[g][0][:, base + j : base + j + 1], (8, 128))
                        for g in range(g0 + j // 8, groups)
                    }
                    for j in range(sb)
                ]
            )
        for p in range(sb):
            gp = g0 + p // 8
            r = p % 8
            for (_, tiles), cols, scale in zip(jobs, columns, scales):
                pivot = jnp.broadcast_to(cols[p][gp][r : r + 1, :], (8, 128))
                inv = 1.0 / pivot
                scale[gp] = jnp.where(iota == r, lax.rsqrt(pivot), scale[gp])
                m = {g: cols[p][g] * inv for g in range(gp, groups)}
                for j in range(p + 1, sb):
                    gj = g0 + j // 8
                    t = jnp.broadcast_to(cols[p][gj][j % 8 : j % 8 + 1, :], (8, 128))
                    for g in range(gj, groups):
                        cols[j][g] = cols[j][g] - m[g] * t
                rows = [jnp.broadcast_to(t[r : r + 1, :], (8, 128)) for t in tiles[gp]]
                for g in range(gp, groups):
                    if g == gp:
                        if r == 7:
                            continue
                        m[g] = jnp.where(iota > r, m[g], 0.0)
                    tiles[g] = [t - m[g] * w for t, w in zip(tiles[g], rows)]
    return [
        [[t * scale[g] for t in tiles[g]] for g in range(groups)] for (_, tiles), scale in zip(jobs, scales)
    ]


def factor_rows(k, reads, u_refs, w_refs, n):
    lanes = lax.broadcasted_iota(jnp.int32, (8, 128), 1)
    sub = lax.broadcasted_iota(jnp.int32, (8, 128), 0)
    nb = PANEL
    lo = k // 128 * 128
    hi = (k + nb - 1) // 128 * 128 + 128
    jobs = []
    for read, u, w in zip(reads, u_refs, w_refs):
        main = read(slice(k, k + nb), slice(lo, n))
        side = jnp.zeros((nb, hi), F32)
        cuts = [0, k - nb, k] if k > nb else [0, k]
        for c0, c1 in zip(cuts, cuts[1:]):
            if c0 < c1:
                col = u[c0:c1, k : k + nb]
                main = main - tn(col, u[c0:c1, lo:n])
                if w is not None:
                    side = side - tn(col, w[c0:c1, 0:hi])
        tiles = []
        for g in range(nb // 8):
            row = [main[8 * g : 8 * g + 8, c : c + 128] for c in range(0, n - lo, 128)]
            if w is not None:
                more = [side[8 * g : 8 * g + 8, c : c + 128] for c in range(0, hi, 128)]
                more[-1] = more[-1] + jnp.where(lanes == sub + (k + 8 * g - (hi - 128)), 1.0, 0.0)
                row += more
            tiles.append(row)
        jobs.append((k, tiles))
    na = (n - lo) // 128
    for tiles, u, w in zip(eliminate(jobs, nb, PIECE), u_refs, w_refs):
        for g in range(nb // 8):
            first = k + 8 * g
            r = slice(first, first + 8)
            for i in range(na):
                c = lo + 128 * i
                t = tiles[g][i]
                if c == lo:
                    t = jnp.where(lanes + c >= sub + first, t, 0.0)
                u[r, c : c + 128] = t
            for c in range(0, lo, 128):
                u[r, c : c + 128] = jnp.zeros((8, 128), F32)
            if w is not None:
                for i, c in enumerate(range(0, hi, 128)):
                    w[r, c : c + 128] = tiles[g][na + i]
                for c in range(hi, n, 128):
                    w[r, c : c + 128] = jnp.zeros((8, 128), F32)


def node_kernel(own, other, out, stacked):
    rank = own.shape[1]
    half = rank // 2
    parity = lax.axis_index("gx") % 2
    gram = 0.25 * (own[0:rank, :] + other[0:rank, :])
    mine = pl.multiple_of(parity * half, half)
    theirs = pl.multiple_of((1 - parity) * half, half)
    stacked[pl.ds(mine, half), :] = own[rank : rank + half, :]
    stacked[pl.ds(theirs, half), :] = other[rank : rank + half, :]
    t = stacked[...]
    right = nn(gram, t)
    out[0:half, :] = 0.25 * tn(t[:, 0:half], right)
    corner = 0.25 * tn(t[:, half:], right[:, half:])
    out[half:, 0:half] = corner[0 : half // 2]
    out[half:, half:] = corner[half // 2 :]


def leaf_kernel(gram, u, w):
    n = gram.shape[1]
    reads = [lambda r, c, m=m: gram[m, r, c] for m in range(2)]
    for k in range(0, n // 2, PANEL):
        factor_rows(k, reads, [u.at[m] for m in range(2)], [w.at[m] for m in range(2)], n)


def orthogonal_kernel(gram, basis, u_half, w_half, q, u, w):
    n = gram.shape[1]
    half = n // 2
    u[:, 0:half, :] = u_half[...]
    w[:, 0:half, :] = w_half[...]
    reads = [lambda r, c, m=m: gram[m, r, c] for m in range(2)]
    for k in range(half, n, PANEL):
        factor_rows(k, reads, [u.at[m] for m in range(2)], [w.at[m] for m in range(2)], n)
    for leaf in range(2):
        rest = w[leaf]
        total = None
        for _ in range(3):
            part = rest.astype(BF16)
            rest = rest - part.astype(F32)
            term = bf_nt(basis[0, leaf], part)
            total = term if total is None else total + term
        q[0, leaf] = total.astype(BF16)


def slot_of(slots, leaf, direction):
    found = 0
    for s in range(5):
        found = found + jnp.where(slots[0, leaf, s] == direction, s, 0)
    return found


def first_kernel(basis_h, transfer_h, node_h, slots_h, points_h, scales_h, tiles_h,
                 gram_h, sent_h, low_h, high_h, up_h, x_h, gx_a, gx_b,
                 gram, sent, acc, basis, transfer, slots, points, scales, tiles, east, west, in_sems, tile_sems, out_sems):
    rank = gram.shape[1]
    half = node_h.shape[2]
    sources = (
        (basis_h, basis), (transfer_h, transfer), (slots_h, slots), (points_h, points), (scales_h, scales),
        (node_h.at[0, 0], sent.at[pl.ds(rank, half)]),
    )
    loads = [pltpu.make_async_copy(a, b, in_sems.at[i]) for i, (a, b) in enumerate(sources)]
    for load in loads:
        load.start()

    def tile_copy(leaf, slot):
        return pltpu.make_async_copy(tiles_h.at[0, leaf, slot], tiles.at[leaf, slot], tile_sems.at[leaf, slot])

    loads[0].wait()
    loads[1].wait()
    for leaf in range(2):
        for slot in range(5):
            tile_copy(leaf, slot).start()
    total = None
    for leaf in range(2):
        b = basis[0, leaf]
        g = dot(b, b, ((0,), (0,)), lax.Precision.DEFAULT) / basis.shape[2]
        gram[leaf] = g
        t = transfer[0, leaf]
        part = tn(t, nn(g, t))
        total = part if total is None else total + part
    sent[0:rank, :] = total
    for load in loads[2:]:
        load.wait()
    waits = []

    def store(scratch, target):
        waits.append(pltpu.make_async_copy(scratch, target, out_sems.at[len(waits)]))
        waits[-1].start()

    store(gram, gram_h)
    store(sent, sent_h)
    west[0] = points[0, 0].T
    west[3] = points[0, 1].T
    east[3] = west[3]
    xt = (west.at[0], west.at[3])
    store(west.at[0], x_h)
    for leaf in range(2):
        for slot in range(5):
            tile_copy(leaf, slot).wait()

    def mirrored(leaf, d):
        slot = slot_of(slots, leaf, d)
        scaled = (xt[leaf][...].astype(F32) * scales[0, slot, pl.ds(leaf, 1), :]).astype(BF16)
        return bf_nn(scaled, tiles[leaf, slot])

    def direct(leaf, d, x):
        slot = slot_of(slots, leaf, d)
        return bf_nt(x, tiles[leaf, slot]) * scales[0, slot, pl.ds(leaf, 1), :]

    east[0] = mirrored(0, 1).astype(BF16)
    west[1] = mirrored(0, 4).astype(BF16)
    east[1] = (mirrored(0, 3) + mirrored(1, 1)).astype(BF16)
    east[2] = mirrored(1, 3).astype(BF16)
    west[2] = mirrored(1, 4).astype(BF16)
    even = lax.axis_index("gx") % 2 == 0

    @pl.when(even)
    def _():
        pltpu.make_async_copy(east, gx_a, out_sems.at[3]).start()
        pltpu.make_async_copy(west, gx_b, out_sems.at[4]).start()

    @pl.when(jnp.logical_not(even))
    def _():
        pltpu.make_async_copy(west, gx_a, out_sems.at[3]).start()
        pltpu.make_async_copy(east, gx_b, out_sems.at[4]).start()

    waits.append(pltpu.make_async_copy(east, gx_a, out_sems.at[3]))
    waits.append(pltpu.make_async_copy(west, gx_b, out_sems.at[4]))
    acc[0] = mirrored(1, 2)
    store(acc.at[0], up_h)
    acc[1] = direct(0, 0, xt[0][...]) + direct(0, 2, xt[1][...])
    store(acc.at[1], low_h)
    acc[2] = direct(1, 0, xt[1][...]) + mirrored(0, 2)
    store(acc.at[2], high_h)
    for w in waits:
        w.wait()


def sides():
    gx, gy = lax.axis_index("gx"), lax.axis_index("gy")
    last_x, last_y = lax.axis_size("gx") - 1, lax.axis_size("gy") - 1
    return gx < last_x, gx > 0, gy < last_y, gy > 0, gx % 2 == 0


def kept(inside, product):
    return jnp.where(inside, product.astype(F32), 0.0)


def up_kernel(own, a, b, out):
    east, west, _, _, even = sides()
    out[...] = (own[...] + a[2].astype(F32) + kept(jnp.where(even, west, east), b[2])).astype(BF16)


def near_top_kernel(slots, scales, tiles, low_in, high_in, gx_a, gx_b, n, n_a, n_b, own, other,
                    out, low_out, top, done, done_sem):
    east, west, north, _, even = sides()
    beside = jnp.where(even, west, east)
    pts = low_in.shape[1]
    order = top.shape[2]
    half = order // 2

    def read(r, c):
        if r.start < half:
            return own[r, c] + other[r, c]
        first = r.start - half
        shift = 0
        if first >= half // 2:
            first, shift = first - half // 2, half
        place = (slice(half + first, half + first + PANEL), slice(shift, shift + half))
        return own[place] + other[place]

    x0_east = jnp.where(even, gx_a[0], gx_b[0])
    x1_east = jnp.where(even, gx_a[3], gx_b[3])
    x1_west = jnp.where(even, gx_b[3], gx_a[3])
    ne = jnp.where(even, n_a[...], n_b[...])
    nw = jnp.where(even, n_b[...], n_a[...])
    terms = (
        ((1, x0_east, east), (3, x1_east, east), (4, x1_west, west)),
        ((1, x1_east, east), (2, n[...], north), (3, ne, north & east), (4, nw, north & west)),
    )
    pieces = [(leaf, c) for leaf in (1, 0) for c in range(0, pts, 128)]
    for i, k in enumerate(range(0, order, PANEL)):
        factor_rows(k, [read], [top.at[0, 0]], [None], order)
        leaf, c = pieces[i]
        cols = slice(c, c + 128)
        if leaf == 0:
            total = low_in[:, cols] + kept(west, jnp.where(even, gx_b[0, :, cols], gx_a[0, :, cols]))
        else:
            total = high_in[:, cols] + gx_a[1, :, cols].astype(F32) + kept(beside, gx_b[1, :, cols])
        for d, x, inside in terms[leaf]:
            slot = slot_of(slots, leaf, d)
            scale = jnp.where(inside, scales[0, slot, pl.ds(leaf, 1), cols], 0.0)
            total = total + bf_nt(x, tiles[0, leaf, slot, cols, :]) * scale
        if leaf == 0:
            low_out[:, cols] = total
        else:
            done[cols, :] = total.T.astype(BF16)
    copy = pltpu.make_async_copy(done, out.at[0, 1], done_sem)
    copy.start()
    copy.wait()


def last_kernel(near, low, south, out, done, sem):
    _, _, _, inside, _ = sides()
    done[...] = (low[...] + kept(inside, south[...])).T.astype(BF16)
    copy = pltpu.make_async_copy(done, out.at[0, 0], sem)
    copy.start()
    copy.wait()


def shape(*dims, dtype=BF16):
    return jax.ShapeDtypeStruct(dims, dtype)


def call(kernel, outs, in_specs, out_specs, scratch=(), flops=10**6, moved=1 << 10, vmem=32 << 20, aliases=None):
    return pl.pallas_call(
        kernel,
        out_shape=outs,
        in_specs=in_specs,
        out_specs=out_specs,
        scratch_shapes=list(scratch),
        input_output_aliases=aliases or {},
        compiler_params=pltpu.CompilerParams(vmem_limit_bytes=vmem),
        cost_estimate=pl.CostEstimate(flops=flops, bytes_accessed=moved, transcendentals=0),
    )


def make_shards(sizes):
    axes = ("gx", "gy")

    def shards(points_x, near_tiles, scales, slot_direction, basis, leaf_transfer, node_transfer):
        pts, vecs = points_x.shape[2:]
        rank = basis.shape[3]
        half = node_transfer.shape[2]
        dma = pltpu.SemaphoreType.DMA

        block = shape(vecs, pts)
        wide = shape(vecs, pts, dtype=F32)
        sides_sent = shape(4, vecs, pts)
        scales = jnp.transpose(scales, (0, 2, 1, 3))
        gram, sent, low, high, up, own_x, gx_a, gx_b = call(
            first_kernel,
            (
                shape(2, rank, rank, dtype=F32),
                shape(rank + half, rank, dtype=F32),
                wide, wide, wide, block, sides_sent, sides_sent,
            ),
            [ANY] * 7,
            (ANY,) * 8,
            [
                pltpu.VMEM((2, rank, rank), F32),
                pltpu.VMEM((rank + half, rank), F32),
                pltpu.VMEM((3, vecs, pts), F32),
                pltpu.VMEM(basis.shape, BF16),
                pltpu.VMEM(leaf_transfer.shape, F32),
                pltpu.SMEM(slot_direction.shape, jnp.int32),
                pltpu.VMEM(points_x.shape, BF16),
                pltpu.VMEM(scales.shape, F32),
                pltpu.VMEM(near_tiles.shape[1:], BF16),
                *[pltpu.VMEM((4, vecs, pts), BF16)] * 2,
                dma((6,)),
                dma((2, 5)),
                dma((8,)),
            ],
        )(*(pltpu.with_memory_space_constraint(a, pltpu.HBM) for a in (
            basis, leaf_transfer, node_transfer, slot_direction, points_x, scales, near_tiles)))
        got = send(sent, axes, sizes, lambda i, j: (i ^ 1, j))

        got_a = send(gx_a, axes, sizes, lambda i, j: (i ^ 1, j))
        got, got_a = lax.optimization_barrier((got, got_a))
        packed = shape(rank - rank // 4, rank, dtype=F32)
        node = call(node_kernel, packed, [VMEM] * 2, VMEM, [pltpu.VMEM((rank, rank), F32)])(sent, got)
        node_got = send(node, axes, sizes, lambda i, j: (i, j ^ 1))
        across = lambda i, j: (i - 1 if i % 2 == 0 else i + 1, j)
        got_b = send(gx_b, axes, sizes, across)
        n = send(own_x, axes, sizes, lambda i, j: (i, j - 1))
        halves = shape(2, rank // 2, rank, dtype=F32)
        u, w = call(leaf_kernel, (halves, halves), [VMEM], (VMEM, VMEM))(gram)

        w, node_got, n = lax.optimization_barrier((w, node_got, n))
        pair = node + node_got
        u, pair = lax.optimization_barrier((u, pair))
        other = send(pair, axes, sizes, lambda i, j: (i ^ 2, j))
        n_a = send(n, axes, sizes, lambda i, j: (i ^ 1, j))
        n_b = send(n, axes, sizes, across)
        square = pltpu.VMEM((2, rank, rank), F32)
        leaf_q = call(orthogonal_kernel, shape(*basis.shape), [VMEM] * 4, VMEM, [square, square])(gram, basis, u, w)

        leaf_q, got_b, other = lax.optimization_barrier((leaf_q, got_b, other))
        total_up = call(up_kernel, block, [VMEM] * 3, VMEM)(up, got_a, got_b)
        south = send(total_up, axes, sizes, lambda i, j: (i, j + 1))

        near, low, top = call(
            near_top_kernel,
            (shape(*points_x.shape), wide, shape(1, 1, rank, rank, dtype=F32)),
            [SMEM, *[VMEM] * 11],
            (ANY, VMEM, VMEM),
            [pltpu.VMEM((pts, vecs), BF16), dma],
        )(slot_direction, scales, near_tiles, low, high, got_a, got_b, n, n_a, n_b, pair, other)
        near = call(
            last_kernel,
            shape(*points_x.shape),
            [ANY, VMEM, VMEM],
            ANY,
            [pltpu.VMEM((pts, vecs), BF16), dma],
            aliases={0: 0},
        )(near, low, south)
        return near, leaf_q, top

    return shards


def solution(mesh):
    leaf = P("gx", "gy", None, None)
    placed = (leaf, P("gx", "gy", None, None, None), leaf, P("gx", "gy", None), leaf, leaf, leaf)
    return jax.shard_map(
        make_shards((mesh.shape["gx"], mesh.shape["gy"])),
        mesh=mesh,
        in_specs=placed,
        out_specs=(leaf, leaf, leaf),
        check_vma=False,
    )
```

```python
import jax
import jax.numpy as jnp
from jax import lax
from jax.experimental import pallas as pl
from jax.experimental.pallas import tpu as pltpu
from jax.sharding import PartitionSpec as P

F32 = jnp.float32
BF16 = jnp.bfloat16
ANY = pl.BlockSpec(memory_space=pl.ANY)
VMEM = pl.BlockSpec(memory_space=pltpu.VMEM)
SMEM = pl.BlockSpec(memory_space=pltpu.SMEM)
PANEL = 32
PIECE = 16
FIRST_ROWS = 160


def dot(a, b, dims, precision=lax.Precision.HIGHEST):
    return lax.dot_general(a, b, (dims, ((), ())), precision=precision, preferred_element_type=F32)


def nn(a, b):
    return dot(a, b, ((1,), (0,)))


def tn(a, b):
    return dot(a, b, ((0,), (0,)))


def bf_nn(a, b):
    return dot(a, b, ((1,), (0,)), lax.Precision.DEFAULT)


def bf_nt(a, b):
    return dot(a, b, ((1,), (1,)), lax.Precision.DEFAULT)


def send(block, axes, sizes, partner):
    count_x, count_y = sizes
    route = []
    for i in range(count_x):
        for j in range(count_y):
            x, y = partner(i, j)
            route.append((i * count_y + j, x % count_x * count_y + y % count_y))
    return lax.ppermute(block, axes, route)


def eliminate(jobs, nb, sb):
    iota = lax.broadcasted_iota(jnp.int32, (8, 128), 0)
    groups = nb // 8
    scales = [[jnp.ones((8, 128), F32) for _ in range(groups)] for _ in jobs]
    for s in range(0, nb, sb):
        g0 = s // 8
        columns = []
        for k, tiles in jobs:
            base = (k + s) % 128
            columns.append(
                [
                    {
                        g: jnp.broadcast_to(tiles[g][0][:, base + j : base + j + 1], (8, 128))
                        for g in range(g0 + j // 8, groups)
                    }
                    for j in range(sb)
                ]
            )
        for p in range(sb):
            gp = g0 + p // 8
            r = p % 8
            for (_, tiles), cols, scale in zip(jobs, columns, scales):
                pivot = jnp.broadcast_to(cols[p][gp][r : r + 1, :], (8, 128))
                inv = 1.0 / pivot
                scale[gp] = jnp.where(iota == r, lax.rsqrt(pivot), scale[gp])
                m = {g: cols[p][g] * inv for g in range(gp, groups)}
                for j in range(p + 1, sb):
                    gj = g0 + j // 8
                    t = jnp.broadcast_to(cols[p][gj][j % 8 : j % 8 + 1, :], (8, 128))
                    for g in range(gj, groups):
                        cols[j][g] = cols[j][g] - m[g] * t
                rows = [jnp.broadcast_to(t[r : r + 1, :], (8, 128)) for t in tiles[gp]]
                for g in range(gp, groups):
                    if g == gp:
                        if r == 7:
                            continue
                        m[g] = jnp.where(iota > r, m[g], 0.0)
                    tiles[g] = [t - m[g] * w for t, w in zip(tiles[g], rows)]
    return [
        [[t * scale[g] for t in tiles[g]] for g in range(groups)] for (_, tiles), scale in zip(jobs, scales)
    ]


def factor_rows(k, reads, u_refs, w_refs, n):
    lanes = lax.broadcasted_iota(jnp.int32, (8, 128), 1)
    sub = lax.broadcasted_iota(jnp.int32, (8, 128), 0)
    nb = PANEL
    lo = k // 128 * 128
    hi = (k + nb - 1) // 128 * 128 + 128
    jobs = []
    for read, u, w in zip(reads, u_refs, w_refs):
        main = read(slice(k, k + nb), slice(lo, n))
        side = jnp.zeros((nb, hi), F32)
        cuts = [0, k - nb, k] if k > nb else [0, k]
        for c0, c1 in zip(cuts, cuts[1:]):
            if c0 < c1:
                col = u[c0:c1, k : k + nb]
                main = main - tn(col, u[c0:c1, lo:n])
                if w is not None:
                    side = side - tn(col, w[c0:c1, 0:hi])
        tiles = []
        for g in range(nb // 8):
            row = [main[8 * g : 8 * g + 8, c : c + 128] for c in range(0, n - lo, 128)]
            if w is not None:
                more = [side[8 * g : 8 * g + 8, c : c + 128] for c in range(0, hi, 128)]
                more[-1] = more[-1] + jnp.where(lanes == sub + (k + 8 * g - (hi - 128)), 1.0, 0.0)
                row += more
            tiles.append(row)
        jobs.append((k, tiles))
    na = (n - lo) // 128
    for tiles, u, w in zip(eliminate(jobs, nb, PIECE), u_refs, w_refs):
        for g in range(nb // 8):
            first = k + 8 * g
            r = slice(first, first + 8)
            for i in range(na):
                c = lo + 128 * i
                t = tiles[g][i]
                if c == lo:
                    t = jnp.where(lanes + c >= sub + first, t, 0.0)
                u[r, c : c + 128] = t
            for c in range(0, lo, 128):
                u[r, c : c + 128] = jnp.zeros((8, 128), F32)
            if w is not None:
                for i, c in enumerate(range(0, hi, 128)):
                    w[r, c : c + 128] = tiles[g][na + i]
                for c in range(hi, n, 128):
                    w[r, c : c + 128] = jnp.zeros((8, 128), F32)


def node_kernel(own, other, out, stacked):
    rank = own.shape[1]
    half = rank // 2
    parity = lax.axis_index("gx") % 2
    gram = 0.25 * (own[0:rank, :] + other[0:rank, :])
    mine = pl.multiple_of(parity * half, half)
    theirs = pl.multiple_of((1 - parity) * half, half)
    stacked[pl.ds(mine, half), :] = own[rank : rank + half, :]
    stacked[pl.ds(theirs, half), :] = other[rank : rank + half, :]
    t = stacked[...]
    right = nn(gram, t)
    out[0:half, :] = 0.25 * tn(t[:, 0:half], right)
    corner = 0.25 * tn(t[:, half:], right[:, half:])
    out[half:, 0:half] = corner[0 : half // 2]
    out[half:, half:] = corner[half // 2 :]


def leaf_kernel(gram, u, w):
    n = gram.shape[1]
    reads = [lambda r, c, m=m: gram[m, r, c] for m in range(2)]
    for k in range(0, FIRST_ROWS, PANEL):
        factor_rows(k, reads, [u.at[m] for m in range(2)], [w.at[m] for m in range(2)], n)


def orthogonal_kernel(gram, basis, u_first, w_first, q, u, w):
    n = gram.shape[1]
    u[:, 0:FIRST_ROWS, :] = u_first[...]
    w[:, 0:FIRST_ROWS, :] = w_first[...]
    reads = [lambda r, c, m=m: gram[m, r, c] for m in range(2)]
    for k in range(FIRST_ROWS, n, PANEL):
        factor_rows(k, reads, [u.at[m] for m in range(2)], [w.at[m] for m in range(2)], n)
    for leaf in range(2):
        rest = w[leaf]
        total = None
        for _ in range(3):
            part = rest.astype(BF16)
            rest = rest - part.astype(F32)
            term = bf_nt(basis[0, leaf], part)
            total = term if total is None else total + term
        q[0, leaf] = total.astype(BF16)


def slot_of(slots, leaf, direction):
    found = 0
    for s in range(5):
        found = found + jnp.where(slots[0, leaf, s] == direction, s, 0)
    return found


def first_kernel(basis_h, transfer_h, node_h, slots_h, points_h, scales_h, tiles_h,
                 gram_h, sent_h, x_h, gx_a, gx_b,
                 gram, sent, basis, transfer, slots, points, scales, tiles, east, west, in_sems, tile_sems, out_sems):
    rank = gram.shape[1]
    half = node_h.shape[2]
    sources = (
        (basis_h, basis), (transfer_h, transfer), (slots_h, slots), (points_h, points), (scales_h, scales),
        (node_h.at[0, 0], sent.at[pl.ds(rank, half)]),
    )
    loads = [pltpu.make_async_copy(a, b, in_sems.at[i]) for i, (a, b) in enumerate(sources)]
    for load in loads:
        load.start()

    def tile_copy(leaf, slot):
        return pltpu.make_async_copy(tiles_h.at[0, leaf, slot], tiles.at[leaf, slot], tile_sems.at[leaf, slot])

    loads[0].wait()
    loads[1].wait()
    for leaf in range(2):
        for slot in range(5):
            tile_copy(leaf, slot).start()
    for leaf in range(2):
        b = basis[0, leaf]
        gram[leaf] = dot(b, b, ((0,), (0,)), lax.Precision.DEFAULT) / basis.shape[2]
    right = [nn(gram[leaf], transfer[0, leaf]) for leaf in range(2)]
    sent[0:rank, :] = tn(transfer[0, 0], right[0]) + tn(transfer[0, 1], right[1])
    for load in loads[2:]:
        load.wait()
    waits = []

    def store(scratch, target):
        waits.append(pltpu.make_async_copy(scratch, target, out_sems.at[len(waits)]))
        waits[-1].start()

    store(gram, gram_h)
    store(sent, sent_h)
    west[0] = points[0, 0].T
    west[3] = points[0, 1].T
    east[3] = west[3]
    xt = (west.at[0], west.at[3])
    store(west.at[0], x_h)
    for leaf in range(2):
        for slot in range(5):
            tile_copy(leaf, slot).wait()

    def mirrored(leaf, d):
        slot = slot_of(slots, leaf, d)
        scaled = (xt[leaf][...].astype(F32) * scales[0, slot, pl.ds(leaf, 1), :]).astype(BF16)
        return bf_nn(scaled, tiles[leaf, slot])

    east[0] = mirrored(0, 1).astype(BF16)
    west[1] = mirrored(0, 4).astype(BF16)
    east[1] = (mirrored(0, 3) + mirrored(1, 1)).astype(BF16)
    east[2] = mirrored(1, 3).astype(BF16)
    west[2] = mirrored(1, 4).astype(BF16)
    even = lax.axis_index("gx") % 2 == 0

    @pl.when(even)
    def _():
        pltpu.make_async_copy(east, gx_a, out_sems.at[3]).start()
        pltpu.make_async_copy(west, gx_b, out_sems.at[4]).start()

    @pl.when(jnp.logical_not(even))
    def _():
        pltpu.make_async_copy(west, gx_a, out_sems.at[3]).start()
        pltpu.make_async_copy(east, gx_b, out_sems.at[4]).start()

    waits.append(pltpu.make_async_copy(east, gx_a, out_sems.at[3]))
    waits.append(pltpu.make_async_copy(west, gx_b, out_sems.at[4]))
    for w in waits:
        w.wait()


def own_kernel(slots, scales, tiles, x0, gx_a, low, high, up):
    xt = (x0[...], gx_a[3])

    def mirrored(leaf, d):
        slot = slot_of(slots, leaf, d)
        scaled = (xt[leaf].astype(F32) * scales[0, slot, pl.ds(leaf, 1), :]).astype(BF16)
        return bf_nn(scaled, tiles[0, leaf, slot])

    def direct(leaf, d, x):
        slot = slot_of(slots, leaf, d)
        return bf_nt(x, tiles[0, leaf, slot]) * scales[0, slot, pl.ds(leaf, 1), :]

    low[...] = direct(0, 0, xt[0]) + direct(0, 2, xt[1])
    high[...] = direct(1, 0, xt[1]) + mirrored(0, 2)
    up[...] = mirrored(1, 2)


def sides():
    gx, gy = lax.axis_index("gx"), lax.axis_index("gy")
    last_x, last_y = lax.axis_size("gx") - 1, lax.axis_size("gy") - 1
    return gx < last_x, gx > 0, gy < last_y, gy > 0, gx % 2 == 0


def kept(inside, product):
    return jnp.where(inside, product.astype(F32), 0.0)


def up_kernel(own, a, b, out):
    east, west, _, _, even = sides()
    out[...] = (own[...] + a[2].astype(F32) + kept(jnp.where(even, west, east), b[2])).astype(BF16)


def near_top_kernel(slots, scales, tiles, low_in, high_in, gx_a, gx_b, n, n_a, n_b, own, other,
                    out, low_out, top, done, done_sem):
    east, west, north, _, even = sides()
    beside = jnp.where(even, west, east)
    pts = low_in.shape[1]
    order = top.shape[2]
    half = order // 2

    def read(r, c):
        if r.start < half:
            return own[r, c] + other[r, c]
        first = r.start - half
        shift = 0
        if first >= half // 2:
            first, shift = first - half // 2, half
        place = (slice(half + first, half + first + PANEL), slice(shift, shift + half))
        return own[place] + other[place]

    x0_east = jnp.where(even, gx_a[0], gx_b[0])
    x1_east = jnp.where(even, gx_a[3], gx_b[3])
    x1_west = jnp.where(even, gx_b[3], gx_a[3])
    ne = jnp.where(even, n_a[...], n_b[...])
    nw = jnp.where(even, n_b[...], n_a[...])
    terms = (
        ((1, x0_east, east), (3, x1_east, east), (4, x1_west, west)),
        ((1, x1_east, east), (2, n[...], north), (3, ne, north & east), (4, nw, north & west)),
    )
    pieces = [(leaf, c) for leaf in (1, 0) for c in range(0, pts, 128)]
    for i, k in enumerate(range(0, order, PANEL)):
        factor_rows(k, [read], [top.at[0, 0]], [None], order)
        leaf, c = pieces[i]
        cols = slice(c, c + 128)
        if leaf == 0:
            total = low_in[:, cols] + kept(west, jnp.where(even, gx_b[0, :, cols], gx_a[0, :, cols]))
        else:
            total = high_in[:, cols] + gx_a[1, :, cols].astype(F32) + kept(beside, gx_b[1, :, cols])
        for d, x, inside in terms[leaf]:
            slot = slot_of(slots, leaf, d)
            scale = jnp.where(inside, scales[0, slot, pl.ds(leaf, 1), cols], 0.0)
            total = total + bf_nt(x, tiles[0, leaf, slot, cols, :]) * scale
        if leaf == 0:
            low_out[:, cols] = total
        else:
            done[cols, :] = total.T.astype(BF16)
    copy = pltpu.make_async_copy(done, out.at[0, 1], done_sem)
    copy.start()
    copy.wait()


def last_kernel(near, low, south, out, done, sem):
    _, _, _, inside, _ = sides()
    done[...] = (low[...] + kept(inside, south[...])).T.astype(BF16)
    copy = pltpu.make_async_copy(done, out.at[0, 0], sem)
    copy.start()
    copy.wait()


def shape(*dims, dtype=BF16):
    return jax.ShapeDtypeStruct(dims, dtype)


def call(kernel, outs, in_specs, out_specs, scratch=(), flops=10**6, moved=1 << 10, vmem=32 << 20, aliases=None):
    return pl.pallas_call(
        kernel,
        out_shape=outs,
        in_specs=in_specs,
        out_specs=out_specs,
        scratch_shapes=list(scratch),
        input_output_aliases=aliases or {},
        compiler_params=pltpu.CompilerParams(vmem_limit_bytes=vmem),
        cost_estimate=pl.CostEstimate(flops=flops, bytes_accessed=moved, transcendentals=0),
    )


def make_shards(sizes):
    axes = ("gx", "gy")

    def shards(points_x, near_tiles, scales, slot_direction, basis, leaf_transfer, node_transfer):
        pts, vecs = points_x.shape[2:]
        rank = basis.shape[3]
        half = node_transfer.shape[2]
        dma = pltpu.SemaphoreType.DMA

        block = shape(vecs, pts)
        wide = shape(vecs, pts, dtype=F32)
        sides_sent = shape(4, vecs, pts)
        scales = jnp.transpose(scales, (0, 2, 1, 3))
        gram, sent, own_x, gx_a, gx_b = call(
            first_kernel,
            (
                shape(2, rank, rank, dtype=F32),
                shape(rank + half, rank, dtype=F32),
                block, sides_sent, sides_sent,
            ),
            [ANY] * 7,
            (ANY,) * 5,
            [
                pltpu.VMEM((2, rank, rank), F32),
                pltpu.VMEM((rank + half, rank), F32),
                pltpu.VMEM(basis.shape, BF16),
                pltpu.VMEM(leaf_transfer.shape, F32),
                pltpu.SMEM(slot_direction.shape, jnp.int32),
                pltpu.VMEM(points_x.shape, BF16),
                pltpu.VMEM(scales.shape, F32),
                pltpu.VMEM(near_tiles.shape[1:], BF16),
                *[pltpu.VMEM((4, vecs, pts), BF16)] * 2,
                dma((6,)),
                dma((2, 5)),
                dma((5,)),
            ],
        )(*(pltpu.with_memory_space_constraint(a, pltpu.HBM) for a in (
            basis, leaf_transfer, node_transfer, slot_direction, points_x, scales, near_tiles)))
        got = send(sent, axes, sizes, lambda i, j: (i ^ 1, j))

        got_a = send(gx_a, axes, sizes, lambda i, j: (i ^ 1, j))
        low, high, up = call(own_kernel, (wide, wide, wide), [SMEM, *[VMEM] * 4], (VMEM, VMEM, VMEM), flops=2 * 10**9)(
            slot_direction, scales, near_tiles, own_x, gx_a)
        got, got_a, low = lax.optimization_barrier((got, got_a, low))
        packed = shape(rank - rank // 4, rank, dtype=F32)
        node = call(node_kernel, packed, [VMEM] * 2, VMEM, [pltpu.VMEM((rank, rank), F32)])(sent, got)
        node_got = send(node, axes, sizes, lambda i, j: (i, j ^ 1))

        def across(i, j):
            other = i - 1 if i % 2 == 0 else i + 1
            return (other, j) if 0 <= other < sizes[0] else (i, j + 1)

        got_b = send(gx_b, axes, sizes, across)
        n = send(own_x, axes, sizes, lambda i, j: (i, j - 1))
        firsts = shape(2, FIRST_ROWS, rank, dtype=F32)
        u, w = call(leaf_kernel, (firsts, firsts), [VMEM], (VMEM, VMEM))(gram)

        w, node_got, n = lax.optimization_barrier((w, node_got, n))
        pair = node + node_got
        u, pair = lax.optimization_barrier((u, pair))
        other = send(pair, axes, sizes, lambda i, j: (i ^ 2, j))
        n_a = send(n, axes, sizes, lambda i, j: (i ^ 1, j))
        n_b = send(n, axes, sizes, across)
        square = pltpu.VMEM((2, rank, rank), F32)
        leaf_q = call(orthogonal_kernel, shape(*basis.shape), [VMEM] * 4, VMEM, [square, square])(gram, basis, u, w)

        leaf_q, got_b, other = lax.optimization_barrier((leaf_q, got_b, other))
        total_up = call(up_kernel, block, [VMEM] * 3, VMEM)(up, got_a, got_b)
        south = send(total_up, axes, sizes, lambda i, j: (i, j + 1))

        near, low, top = call(
            near_top_kernel,
            (shape(*points_x.shape), wide, shape(1, 1, rank, rank, dtype=F32)),
            [SMEM, *[VMEM] * 11],
            (ANY, VMEM, VMEM),
            [pltpu.VMEM((pts, vecs), BF16), dma],
        )(slot_direction, scales, near_tiles, low, high, got_a, got_b, n, n_a, n_b, pair, other)
        near = call(
            last_kernel,
            shape(*points_x.shape),
            [ANY, VMEM, VMEM],
            ANY,
            [pltpu.VMEM((pts, vecs), BF16), dma],
            aliases={0: 0},
        )(near, low, south)
        return near, leaf_q, top

    return shards


def solution(mesh):
    leaf = P("gx", "gy", None, None)
    placed = (leaf, P("gx", "gy", None, None, None), leaf, P("gx", "gy", None), leaf, leaf, leaf)
    return jax.shard_map(
        make_shards((mesh.shape["gx"], mesh.shape["gy"])),
        mesh=mesh,
        in_specs=placed,
        out_specs=(leaf, leaf, leaf),
        check_vma=False,
    )
```

```python
import jax
import jax.numpy as jnp
from jax import lax
from jax.experimental import pallas as pl
from jax.experimental.pallas import tpu as pltpu
from jax.sharding import PartitionSpec as P

F32 = jnp.float32
BF16 = jnp.bfloat16
ANY = pl.BlockSpec(memory_space=pl.ANY)
VMEM = pl.BlockSpec(memory_space=pltpu.VMEM)
SMEM = pl.BlockSpec(memory_space=pltpu.SMEM)
PANEL = 32
PIECE = 16
FIRST_ROWS = 192


def dot(a, b, dims, precision=lax.Precision.HIGHEST):
    return lax.dot_general(a, b, (dims, ((), ())), precision=precision, preferred_element_type=F32)


def nn(a, b):
    return dot(a, b, ((1,), (0,)))


def tn(a, b):
    return dot(a, b, ((0,), (0,)))


def bf_nn(a, b):
    return dot(a, b, ((1,), (0,)), lax.Precision.DEFAULT)


def bf_nt(a, b):
    return dot(a, b, ((1,), (1,)), lax.Precision.DEFAULT)


def send(block, axes, sizes, partner):
    count_x, count_y = sizes
    route = []
    for i in range(count_x):
        for j in range(count_y):
            x, y = partner(i, j)
            route.append((i * count_y + j, x % count_x * count_y + y % count_y))
    return lax.ppermute(block, axes, route)


def eliminate(jobs, nb, sb):
    iota = lax.broadcasted_iota(jnp.int32, (8, 128), 0)
    groups = nb // 8
    scales = [[jnp.ones((8, 128), F32) for _ in range(groups)] for _ in jobs]
    for s in range(0, nb, sb):
        g0 = s // 8
        columns = []
        for k, tiles in jobs:
            base = (k + s) % 128
            columns.append(
                [
                    {
                        g: jnp.broadcast_to(tiles[g][0][:, base + j : base + j + 1], (8, 128))
                        for g in range(g0 + j // 8, groups)
                    }
                    for j in range(sb)
                ]
            )
        for p in range(sb):
            gp = g0 + p // 8
            r = p % 8
            for (_, tiles), cols, scale in zip(jobs, columns, scales):
                pivot = jnp.broadcast_to(cols[p][gp][r : r + 1, :], (8, 128))
                inv = 1.0 / pivot
                scale[gp] = jnp.where(iota == r, lax.rsqrt(pivot), scale[gp])
                m = {g: cols[p][g] * inv for g in range(gp, groups)}
                for j in range(p + 1, sb):
                    gj = g0 + j // 8
                    t = jnp.broadcast_to(cols[p][gj][j % 8 : j % 8 + 1, :], (8, 128))
                    for g in range(gj, groups):
                        cols[j][g] = cols[j][g] - m[g] * t
                rows = [jnp.broadcast_to(t[r : r + 1, :], (8, 128)) for t in tiles[gp]]
                for g in range(gp, groups):
                    if g == gp:
                        if r == 7:
                            continue
                        m[g] = jnp.where(iota > r, m[g], 0.0)
                    tiles[g] = [t - m[g] * w for t, w in zip(tiles[g], rows)]
    return [
        [[t * scale[g] for t in tiles[g]] for g in range(groups)] for (_, tiles), scale in zip(jobs, scales)
    ]


def factor_rows(k, reads, u_refs, w_refs, n):
    lanes = lax.broadcasted_iota(jnp.int32, (8, 128), 1)
    sub = lax.broadcasted_iota(jnp.int32, (8, 128), 0)
    nb = PANEL
    lo = k // 128 * 128
    hi = (k + nb - 1) // 128 * 128 + 128
    jobs = []
    for read, u, w in zip(reads, u_refs, w_refs):
        main = read(slice(k, k + nb), slice(lo, n))
        side = jnp.zeros((nb, hi), F32)
        cuts = [0, k - nb, k] if k > nb else [0, k]
        for c0, c1 in zip(cuts, cuts[1:]):
            if c0 < c1:
                col = u[c0:c1, k : k + nb]
                main = main - tn(col, u[c0:c1, lo:n])
                if w is not None:
                    side = side - tn(col, w[c0:c1, 0:hi])
        tiles = []
        for g in range(nb // 8):
            row = [main[8 * g : 8 * g + 8, c : c + 128] for c in range(0, n - lo, 128)]
            if w is not None:
                more = [side[8 * g : 8 * g + 8, c : c + 128] for c in range(0, hi, 128)]
                more[-1] = more[-1] + jnp.where(lanes == sub + (k + 8 * g - (hi - 128)), 1.0, 0.0)
                row += more
            tiles.append(row)
        jobs.append((k, tiles))
    na = (n - lo) // 128
    for tiles, u, w in zip(eliminate(jobs, nb, PIECE), u_refs, w_refs):
        for g in range(nb // 8):
            first = k + 8 * g
            r = slice(first, first + 8)
            for i in range(na):
                c = lo + 128 * i
                t = tiles[g][i]
                if c == lo:
                    t = jnp.where(lanes + c >= sub + first, t, 0.0)
                u[r, c : c + 128] = t
            for c in range(0, lo, 128):
                u[r, c : c + 128] = jnp.zeros((8, 128), F32)
            if w is not None:
                for i, c in enumerate(range(0, hi, 128)):
                    w[r, c : c + 128] = tiles[g][na + i]
                for c in range(hi, n, 128):
                    w[r, c : c + 128] = jnp.zeros((8, 128), F32)


def node_kernel(own, other, out, stacked):
    rank = own.shape[1]
    half = rank // 2
    parity = lax.axis_index("gx") % 2
    gram = 0.25 * (own[0:rank, :] + other[0:rank, :])
    mine = pl.multiple_of(parity * half, half)
    theirs = pl.multiple_of((1 - parity) * half, half)
    stacked[pl.ds(mine, half), :] = own[rank : rank + half, :]
    stacked[pl.ds(theirs, half), :] = other[rank : rank + half, :]
    t = stacked[...]
    right = nn(gram, t)
    out[0:half, :] = 0.25 * tn(t[:, 0:half], right)
    corner = 0.25 * tn(t[:, half:], right[:, half:])
    out[half:, 0:half] = corner[0 : half // 2]
    out[half:, half:] = corner[half // 2 :]


def leaf_kernel(gram, u, w):
    n = gram.shape[1]
    reads = [lambda r, c, m=m: gram[m, r, c] for m in range(2)]
    for k in range(0, FIRST_ROWS, PANEL):
        factor_rows(k, reads, [u.at[m] for m in range(2)], [w.at[m] for m in range(2)], n)


def orthogonal_kernel(gram, basis, u_first, w_first, q, u, w):
    n = gram.shape[1]
    u[:, 0:FIRST_ROWS, :] = u_first[...]
    w[:, 0:FIRST_ROWS, :] = w_first[...]
    reads = [lambda r, c, m=m: gram[m, r, c] for m in range(2)]

    def orthogonal(first, last):
        for leaf in range(2):
            rest = w[leaf, first:last, 0:last]
            total = None
            for _ in range(3):
                part = rest.astype(BF16)
                rest = rest - part.astype(F32)
                term = bf_nt(basis[0, leaf, :, 0:last], part)
                total = term if total is None else total + term
            q[0, leaf, :, first:last] = total.astype(BF16)

    for k in range(FIRST_ROWS, n, PANEL):
        factor_rows(k, reads, [u.at[m] for m in range(2)], [w.at[m] for m in range(2)], n)
        if k == FIRST_ROWS:
            orthogonal(0, n // 2)
    orthogonal(n // 2, n)


def slot_of(slots, leaf, direction):
    found = 0
    for s in range(5):
        found = found + jnp.where(slots[0, leaf, s] == direction, s, 0)
    return found


def first_kernel(basis_h, transfer_h, node_h, slots_h, points_h, scales_h, tiles_h,
                 gram_h, sent_h, x_h, gx_a, gx_b,
                 gram, sent, basis, transfer, slots, points, scales, tiles, east, west, in_sems, tile_sems, out_sems):
    rank = gram.shape[1]
    half = node_h.shape[2]
    sources = (
        (basis_h, basis), (transfer_h, transfer), (slots_h, slots), (points_h, points), (scales_h, scales),
        (node_h.at[0, 0], sent.at[pl.ds(rank, half)]),
    )
    loads = [pltpu.make_async_copy(a, b, in_sems.at[i]) for i, (a, b) in enumerate(sources)]
    for load in loads:
        load.start()

    def tile_copy(leaf, slot):
        return pltpu.make_async_copy(tiles_h.at[0, leaf, slot], tiles.at[leaf, slot], tile_sems.at[leaf, slot])

    loads[0].wait()
    loads[1].wait()
    for leaf in range(2):
        for slot in range(5):
            tile_copy(leaf, slot).start()
    for leaf in range(2):
        b = basis[0, leaf]
        gram[leaf] = dot(b, b, ((0,), (0,)), lax.Precision.DEFAULT) / basis.shape[2]
    right = [nn(gram[leaf], transfer[0, leaf]) for leaf in range(2)]
    sent[0:rank, :] = tn(transfer[0, 0], right[0]) + tn(transfer[0, 1], right[1])
    for load in loads[2:]:
        load.wait()
    waits = []

    def store(scratch, target):
        waits.append(pltpu.make_async_copy(scratch, target, out_sems.at[len(waits)]))
        waits[-1].start()

    store(gram, gram_h)
    store(sent, sent_h)
    west[0] = points[0, 0].T
    west[3] = points[0, 1].T
    east[3] = west[3]
    xt = (west.at[0], west.at[3])
    store(west.at[0], x_h)
    for leaf in range(2):
        for slot in range(5):
            tile_copy(leaf, slot).wait()

    def mirrored(leaf, d):
        slot = slot_of(slots, leaf, d)
        scaled = (xt[leaf][...].astype(F32) * scales[0, slot, pl.ds(leaf, 1), :]).astype(BF16)
        return bf_nn(scaled, tiles[leaf, slot])

    east[0] = mirrored(0, 1).astype(BF16)
    west[1] = mirrored(0, 4).astype(BF16)
    east[1] = (mirrored(0, 3) + mirrored(1, 1)).astype(BF16)
    east[2] = mirrored(1, 3).astype(BF16)
    west[2] = mirrored(1, 4).astype(BF16)
    even = lax.axis_index("gx") % 2 == 0

    @pl.when(even)
    def _():
        pltpu.make_async_copy(east, gx_a, out_sems.at[3]).start()
        pltpu.make_async_copy(west, gx_b, out_sems.at[4]).start()

    @pl.when(jnp.logical_not(even))
    def _():
        pltpu.make_async_copy(west, gx_a, out_sems.at[3]).start()
        pltpu.make_async_copy(east, gx_b, out_sems.at[4]).start()

    waits.append(pltpu.make_async_copy(east, gx_a, out_sems.at[3]))
    waits.append(pltpu.make_async_copy(west, gx_b, out_sems.at[4]))
    for w in waits:
        w.wait()


def own_kernel(slots, scales, tiles, x0, gx_a, low, high, up):
    xt = (x0[...], gx_a[3])

    def mirrored(leaf, d):
        slot = slot_of(slots, leaf, d)
        scaled = (xt[leaf].astype(F32) * scales[0, slot, pl.ds(leaf, 1), :]).astype(BF16)
        return bf_nn(scaled, tiles[0, leaf, slot])

    def direct(leaf, d, x):
        slot = slot_of(slots, leaf, d)
        return bf_nt(x, tiles[0, leaf, slot]) * scales[0, slot, pl.ds(leaf, 1), :]

    low[...] = direct(0, 0, xt[0]) + direct(0, 2, xt[1])
    high[...] = direct(1, 0, xt[1]) + mirrored(0, 2)
    up[...] = mirrored(1, 2)


def sides():
    gx, gy = lax.axis_index("gx"), lax.axis_index("gy")
    last_x, last_y = lax.axis_size("gx") - 1, lax.axis_size("gy") - 1
    return gx < last_x, gx > 0, gy < last_y, gy > 0, gx % 2 == 0


def kept(inside, product):
    return jnp.where(inside, product.astype(F32), 0.0)


def up_kernel(own, a, b, out):
    east, west, _, _, even = sides()
    out[...] = (own[...] + a[2].astype(F32) + kept(jnp.where(even, west, east), b[2])).astype(BF16)


def near_top_kernel(slots, scales, tiles, low_in, high_in, gx_a, gx_b, n, n_a, n_b, own, other,
                    out, low_out, top, done, done_sem):
    east, west, north, _, even = sides()
    beside = jnp.where(even, west, east)
    pts = low_in.shape[1]
    order = top.shape[2]
    half = order // 2

    def read(r, c):
        if r.start < half:
            return own[r, c] + other[r, c]
        first = r.start - half
        shift = 0
        if first >= half // 2:
            first, shift = first - half // 2, half
        place = (slice(half + first, half + first + PANEL), slice(shift, shift + half))
        return own[place] + other[place]

    x0_east = jnp.where(even, gx_a[0], gx_b[0])
    x1_east = jnp.where(even, gx_a[3], gx_b[3])
    x1_west = jnp.where(even, gx_b[3], gx_a[3])
    ne = jnp.where(even, n_a[...], n_b[...])
    nw = jnp.where(even, n_b[...], n_a[...])
    terms = (
        ((1, x0_east, east), (3, x1_east, east), (4, x1_west, west)),
        ((1, x1_east, east), (2, n[...], north), (3, ne, north & east), (4, nw, north & west)),
    )
    pieces = [(leaf, c) for leaf in (1, 0) for c in range(0, pts, 128)]
    for i, k in enumerate(range(0, order, PANEL)):
        factor_rows(k, [read], [top.at[0, 0]], [None], order)
        leaf, c = pieces[i]
        cols = slice(c, c + 128)
        if leaf == 0:
            total = low_in[:, cols] + kept(west, jnp.where(even, gx_b[0, :, cols], gx_a[0, :, cols]))
        else:
            total = high_in[:, cols] + gx_a[1, :, cols].astype(F32) + kept(beside, gx_b[1, :, cols])
        for d, x, inside in terms[leaf]:
            slot = slot_of(slots, leaf, d)
            scale = jnp.where(inside, scales[0, slot, pl.ds(leaf, 1), cols], 0.0)
            total = total + bf_nt(x, tiles[0, leaf, slot, cols, :]) * scale
        if leaf == 0:
            low_out[:, cols] = total
        else:
            done[cols, :] = total.T.astype(BF16)
    copy = pltpu.make_async_copy(done, out.at[0, 1], done_sem)
    copy.start()
    copy.wait()


def last_kernel(near, low, south, out, done, sem):
    _, _, _, inside, _ = sides()
    done[...] = (low[...] + kept(inside, south[...])).T.astype(BF16)
    copy = pltpu.make_async_copy(done, out.at[0, 0], sem)
    copy.start()
    copy.wait()


def shape(*dims, dtype=BF16):
    return jax.ShapeDtypeStruct(dims, dtype)


def call(kernel, outs, in_specs, out_specs, scratch=(), flops=10**6, moved=1 << 10, vmem=32 << 20, aliases=None):
    return pl.pallas_call(
        kernel,
        out_shape=outs,
        in_specs=in_specs,
        out_specs=out_specs,
        scratch_shapes=list(scratch),
        input_output_aliases=aliases or {},
        compiler_params=pltpu.CompilerParams(vmem_limit_bytes=vmem),
        cost_estimate=pl.CostEstimate(flops=flops, bytes_accessed=moved, transcendentals=0),
    )


def make_shards(sizes):
    axes = ("gx", "gy")

    def shards(points_x, near_tiles, scales, slot_direction, basis, leaf_transfer, node_transfer):
        pts, vecs = points_x.shape[2:]
        rank = basis.shape[3]
        half = node_transfer.shape[2]
        dma = pltpu.SemaphoreType.DMA

        block = shape(vecs, pts)
        wide = shape(vecs, pts, dtype=F32)
        sides_sent = shape(4, vecs, pts)
        scales = jnp.transpose(scales, (0, 2, 1, 3))
        gram, sent, own_x, gx_a, gx_b = call(
            first_kernel,
            (
                shape(2, rank, rank, dtype=F32),
                shape(rank + half, rank, dtype=F32),
                block, sides_sent, sides_sent,
            ),
            [ANY] * 7,
            (ANY,) * 5,
            [
                pltpu.VMEM((2, rank, rank), F32),
                pltpu.VMEM((rank + half, rank), F32),
                pltpu.VMEM(basis.shape, BF16),
                pltpu.VMEM(leaf_transfer.shape, F32),
                pltpu.SMEM(slot_direction.shape, jnp.int32),
                pltpu.VMEM(points_x.shape, BF16),
                pltpu.VMEM(scales.shape, F32),
                pltpu.VMEM(near_tiles.shape[1:], BF16),
                *[pltpu.VMEM((4, vecs, pts), BF16)] * 2,
                dma((6,)),
                dma((2, 5)),
                dma((5,)),
            ],
        )(*(pltpu.with_memory_space_constraint(a, pltpu.HBM) for a in (
            basis, leaf_transfer, node_transfer, slot_direction, points_x, scales, near_tiles)))
        got = send(sent, axes, sizes, lambda i, j: (i ^ 1, j))

        got_a = send(gx_a, axes, sizes, lambda i, j: (i ^ 1, j))
        low, high, up = call(own_kernel, (wide, wide, wide), [SMEM, *[VMEM] * 4], (VMEM, VMEM, VMEM), flops=2 * 10**9)(
            slot_direction, scales, near_tiles, own_x, gx_a)
        got, got_a, low = lax.optimization_barrier((got, got_a, low))
        packed = shape(rank - rank // 4, rank, dtype=F32)
        node = call(node_kernel, packed, [VMEM] * 2, VMEM, [pltpu.VMEM((rank, rank), F32)])(sent, got)
        node_got = send(node, axes, sizes, lambda i, j: (i, j ^ 1))

        def across(i, j):
            other = i - 1 if i % 2 == 0 else i + 1
            return (other, j) if 0 <= other < sizes[0] else (i, j + 1)

        got_b = send(gx_b, axes, sizes, across)
        n = send(own_x, axes, sizes, lambda i, j: (i, j - 1))
        firsts = shape(2, FIRST_ROWS, rank, dtype=F32)
        u, w = call(leaf_kernel, (firsts, firsts), [VMEM], (VMEM, VMEM))(gram)

        w, node_got, n = lax.optimization_barrier((w, node_got, n))
        pair = node + node_got
        u, pair = lax.optimization_barrier((u, pair))
        other = send(pair, axes, sizes, lambda i, j: (i ^ 2, j))
        n_a = send(n, axes, sizes, lambda i, j: (i ^ 1, j))
        n_b = send(n, axes, sizes, across)
        square = pltpu.VMEM((2, rank, rank), F32)
        leaf_q = call(orthogonal_kernel, shape(*basis.shape), [VMEM] * 4, VMEM, [square, square])(gram, basis, u, w)

        leaf_q, got_b, other = lax.optimization_barrier((leaf_q, got_b, other))
        total_up = call(up_kernel, block, [VMEM] * 3, VMEM)(up, got_a, got_b)
        south = send(total_up, axes, sizes, lambda i, j: (i, j + 1))

        near, low, top = call(
            near_top_kernel,
            (shape(*points_x.shape), wide, shape(1, 1, rank, rank, dtype=F32)),
            [SMEM, *[VMEM] * 11],
            (ANY, VMEM, VMEM),
            [pltpu.VMEM((pts, vecs), BF16), dma],
        )(slot_direction, scales, near_tiles, low, high, got_a, got_b, n, n_a, n_b, pair, other)
        near = call(
            last_kernel,
            shape(*points_x.shape),
            [ANY, VMEM, VMEM],
            ANY,
            [pltpu.VMEM((pts, vecs), BF16), dma],
            aliases={0: 0},
        )(near, low, south)
        return near, leaf_q, top

    return shards


def solution(mesh):
    leaf = P("gx", "gy", None, None)
    placed = (leaf, P("gx", "gy", None, None, None), leaf, P("gx", "gy", None), leaf, leaf, leaf)
    return jax.shard_map(
        make_shards((mesh.shape["gx"], mesh.shape["gy"])),
        mesh=mesh,
        in_specs=placed,
        out_specs=(leaf, leaf, leaf),
        check_vma=False,
    )
```
